512 devices in a mesh: leaf: 32 (over z, core), frow: 4 (over x), fcol: 4 (over y).
Axes of the slice: x: 4, y: 4, z: 16, core: 2. Of those that a mesh axis runs over, the one named last changes fastest.
Arguments:
- child_update: float32 [32, 3584, 3584], P('leaf', 'frow', 'fcol'), may hold values from -0.5 to 5, as said below
- own_part: float32 [32, 2, 512, 512], P('leaf', None, 'frow', 'fcol'), may hold values from -0.5 to 1.5, as said below
- child_maps: int32 [48, 4, 7], replicated, may hold values from 0 to 7, as said below
Outputs:
- factor_panel: float32 [32, 4096, 512], P('leaf', 'frow', 'fcol')
The draws below stay inside these ranges and needn't reach their ends.
Inputs may be any that keep to these rules, and one draw needn't show every extreme that they name: child_maps[c, q] lists 7 distinct parent block numbers of quarter q in increasing order. Each child_update[i] is symmetric positive definite. Each own_part[i, l] is symmetric positive definite.
All inputs are finite; a program needn't handle non-finite values.
Results may differ from the reference program's by a relative error of at most 0.0003.
Values sent between devices are 32-bit elements; how exact they have to be, the bound alone decides.
A program may use at most 128 MiB of HBM per device.

```python
import math
import jax
import jax.numpy as jnp
from jax import lax

BLOCK = 128
F = 4096
P_SIZE = 512
SUBTREES = 32
QUARTERS = 4
MERGES = 2
CHILDREN = 48
M = 3584
FL = 1024
PL = 128
ML = 896
FBL = 8
MBL = 7


coherent_weight = 10.0


def definite_matrix(key_in, order, lowest, highest):
    first, second, third = jax.random.split(key_in, 3)
    spread = math.sqrt(3.0) * 0.3 / math.sqrt(order)
    noise = jax.random.uniform(first, (order, order), jnp.float32, -spread, spread)
    symmetric = (noise + noise.T) * (1.0 / math.sqrt(2.0))
    positions = jnp.arange(order)
    diagonal_mask = positions[:, None] == positions[None, :]
    unit_matrix = jnp.where(diagonal_mask, jnp.float32(1.0), symmetric)
    profile = jax.random.uniform(third, (order,), jnp.float32, 0.5, 1.5)
    unit_matrix = unit_matrix + coherent_weight / order * profile[:, None] * profile[None, :]
    logs = jax.random.uniform(second, (order,), jnp.float32, math.log(lowest), math.log(highest))
    roots = jnp.sqrt(jnp.exp(logs))
    return unit_matrix * roots[:, None] * roots[None, :]


def draw_child_update(key, part):
    key = jax.random.fold_in(key, 1)
    subkeys = jax.random.split(key, SUBTREES)
    lowest, highest = (0.8, 1.25)
    return lax.map(lambda subkey: definite_matrix(subkey, M, lowest, highest), subkeys)


def draw_own_part(key, part):
    key = jax.random.fold_in(key, 2)
    subkeys = jax.random.split(key, SUBTREES * MERGES)
    lowest, highest = (0.3, 0.6)
    drawn = lax.map(lambda subkey: definite_matrix(subkey, P_SIZE, lowest, highest), subkeys)
    return drawn.reshape(SUBTREES, MERGES, P_SIZE, P_SIZE)


def draw_child_maps(key, part):
    key = jax.random.fold_in(key, 3)
    subkeys = jax.random.split(key, CHILDREN * QUARTERS)
    chosen = jax.vmap(lambda subkey: jnp.sort(jax.random.permutation(subkey, FBL)[:MBL]))(subkeys)
    return chosen.reshape(CHILDREN, QUARTERS, MBL).astype(jnp.int32)


def setup_inputs(seed: int = 0) -> dict:
    arg_keys = jax.random.split(jax.random.key(seed), 4)
    child_update = draw_child_update(jax.random.fold_in(arg_keys[3], 71), 0)
    own_part = draw_own_part(jax.random.fold_in(arg_keys[3], 71), 0)
    child_maps = draw_child_maps(jax.random.fold_in(arg_keys[3], 71), 0)
    return {"child_update": child_update, "own_part": own_part, "child_maps": child_maps}


def quarter_inverse(node_maps):
    quarter_count = node_maps.shape[0]
    child_blocks = node_maps.shape[1]
    parent_slots = jnp.arange(FBL, dtype=jnp.int32)
    matches = node_maps[:, None, :] == parent_slots[None, :, None]
    present = jnp.any(matches, axis=2)
    child_slot = jnp.argmax(matches.astype(jnp.int32), axis=2).astype(jnp.int32)
    offsets = (jnp.arange(quarter_count, dtype=jnp.int32) * child_blocks)[:, None]
    missing = jnp.int32(quarter_count * child_blocks)
    return jnp.where(present, child_slot + offsets, missing).reshape(-1).astype(jnp.int32)

def extend(update_matrix, node_maps):
    block_order = quarter_inverse(node_maps)
    block_count = update_matrix.shape[0] // BLOCK
    blocks = update_matrix.reshape(block_count, BLOCK, block_count, BLOCK)
    blocks = jnp.pad(blocks, ((0, 1), (0, 0), (0, 1), (0, 0)))
    placed = jnp.take(blocks, block_order, axis=0)
    placed = jnp.take(placed, block_order, axis=2)
    return placed.reshape(F, F)

def reference(child_update, own_part, child_maps):
    updates = child_update
    map_offset = 0
    for merge_level in range(1, MERGES + 1):
        node_count = SUBTREES // 2 ** merge_level
        group_width = 2 ** merge_level
        own_sums = jnp.sum(own_part[:, merge_level - 1].reshape(node_count, group_width, P_SIZE, P_SIZE), axis=1)
        node_maps = child_maps[map_offset:map_offset + 2 * node_count].reshape(node_count, 2, QUARTERS, MBL)
        pair_updates = updates.reshape(node_count, 2, M, M)
        is_top = merge_level == MERGES

        def assemble(operands):
            pair_now, pair_maps, own_block = operands
            front_matrix = extend(pair_now[0], pair_maps[0]) + extend(pair_now[1], pair_maps[1])
            front_quarters = front_matrix.reshape(QUARTERS, FL, QUARTERS, FL)
            front_quarters = front_quarters.at[:, :PL, :, :PL].add(own_block.reshape(QUARTERS, PL, QUARTERS, PL))
            pivot_matrix = front_quarters[:, :PL, :, :PL].reshape(P_SIZE, P_SIZE)
            below_pivot = front_quarters[:, PL:, :, :PL].reshape(M, P_SIZE)
            pivot_factor = jnp.linalg.cholesky(pivot_matrix)
            below_factor = lax.linalg.triangular_solve(pivot_factor, below_pivot, left_side=False, lower=True, transpose_a=True)
            if is_top:
                panel_rows = jnp.concatenate([pivot_factor.reshape(QUARTERS, PL, P_SIZE), below_factor.reshape(QUARTERS, ML, P_SIZE)], axis=1)
                return panel_rows.reshape(F, P_SIZE)
            trailing = front_quarters[:, PL:, :, PL:].reshape(M, M)
            product = lax.dot_general(below_factor.astype(jnp.float32), below_factor.astype(jnp.float32), (((1,), (1,)), ((), ())), precision=lax.Precision.HIGHEST, preferred_element_type=jnp.float32)
            return trailing - product
        updates = lax.map(assemble, (pair_updates, node_maps, own_sums))
        map_offset = map_offset + 2 * node_count
    return jnp.repeat(updates, 2 ** MERGES, axis=0)
```

```python
import jax
import jax.numpy as jnp
from jax import lax
from jax.experimental import pallas as pl
from jax.experimental.pallas import tpu as pltpu
from jax.sharding import PartitionSpec as P

HI = lax.Precision.HIGHEST
MESH = pl.DeviceIdType.MESH


def mm(a, b, ca, cb):
    return lax.dot_general(a, b, (((ca,), (cb,)), ((), ())), precision=HI, preferred_element_type=jnp.float32)

def bc(x):
    return jnp.broadcast_to(x, (8, 128))

def small_factor(cols):
    a = {}
    for j in range(8):
        for i in range(j, 8):
            a[i, j] = bc(cols[j][i:i + 1, :])
    low, inv, x = {}, {}, {}
    for j in range(8):
        inv[j] = lax.rsqrt(a[j, j])
        for i in range(j + 1, 8):
            low[i, j] = a[i, j] * inv[j]
        for k in range(j + 1, 8):
            for i in range(k, 8):
                a[i, k] = a[i, k] - low[i, j] * low[k, j]
    for j in range(8):
        x[j, j] = inv[j]
        for i in range(j + 1, 8):
            t = low[i, j] * x[j, j]
            for k in range(j + 1, i):
                t = t + low[i, k] * x[k, j]
            x[i, j] = -(inv[i] * t)
    return x

def tree(terms):
    while len(terms) > 1:
        terms = [terms[i] + terms[i + 1] if i + 1 < len(terms) else terms[i] for i in range(0, len(terms), 2)]
    return terms[0]

def diag_factor(read, write_x, write_u):
    lane = lax.broadcasted_iota(jnp.int32, (8, 128), 1)
    sub = lax.broadcasted_iota(jnp.int32, (8, 128), 0)
    rows = [read(i) for i in range(16)]
    for s in range(16):
        base = 8 * s
        top = rows[s]
        here = (lane >= base) & (lane < base + 8)
        cols = [bc(top[:, base + j:base + j + 1]) for j in range(8)]
        x = small_factor(cols)
        p = []
        for j in range(8):
            v = x[7, j]
            for i in range(6, j - 1, -1):
                v = jnp.where(sub <= i, x[i, j], v)
            p.append(jnp.where(sub >= j, v, 0.0) if j else v)
        q = []
        for j in range(8):
            v = x[j, j]
            for i in range(j - 1, -1, -1):
                v = jnp.where(sub <= i, x[j, i], v)
            q.append(jnp.where(sub <= j, v, 0.0) if j < 7 else v)
        unit = jnp.where(here, (lane - base == sub).astype(jnp.float32), top)
        w = tree([p[j] * bc(unit[j:j + 1, :]) for j in range(8)])
        write_x(s, jnp.where(lane < base + 8, w, 0.0))
        if write_u is not None:
            u = tree([p[j] * bc(top[j:j + 1, :]) for j in range(8)])
            write_u(s, jnp.where(lane - base >= sub, u, 0.0))
        if s == 15:
            break
        g = tree([q[j] * bc(w[j:j + 1, :]) for j in range(8)])
        gr = [bc(g[j:j + 1, :]) for j in range(8)]
        for i in range(s + 1, 16):
            m = [bc(rows[i][:, base + j:base + j + 1]) for j in range(8)]
            rows[i] = jnp.where(here, 0.0, rows[i]) - tree([m[j] * gr[j] for j in range(8)])

def block_factor(s_ref, x_ref, u_ref, width, z_ref=None):
    def step(j, _):
        cj = pl.multiple_of(j * 128, 128)
        def wx(s, v):
            x_ref[8 * s:8 * s + 8, :] = v
        def wu(s, v):
            u_ref[j, 8 * s:8 * s + 8, :] = v
        diag_factor(lambda i: s_ref[j, 8 * i:8 * i + 8, pl.ds(cj, 128)], wx, wu if u_ref is not None else None)
        r_i = lax.broadcasted_iota(jnp.int32, (128, 128), 0)
        c_i = lax.broadcasted_iota(jnp.int32, (128, 128), 1)
        s_ref[j, :, pl.ds(cj, 128)] = (r_i == c_i).astype(jnp.float32)
        s_ref[j] = mm(x_ref[...], s_ref[j], 1, 0)
        def trail(i, _):
            ci = pl.multiple_of(i * 128, 128)
            s_ref[i, :, pl.ds(cj, 128)] = jnp.zeros((128, 128), jnp.float32)
            s_ref[i] = s_ref[i] - mm(s_ref[j, :, pl.ds(ci, 128)], s_ref[j], 0, 0)
            return 0
        lax.fori_loop(j + 1, 4, trail, 0)
        if z_ref is not None:
            lanes = lax.broadcasted_iota(jnp.int32, (128, 512), 1)
            li = jnp.where(lanes < (j + 1) * 128, s_ref[j, :, :512], 0.0)
            z_ref[...] += mm(li, s_ref[j, :, 512:640], 0, 0)
        return 0
    if z_ref is not None:
        z_ref[...] = jnp.zeros_like(z_ref)
    lax.fori_loop(0, 4, step, 0)


def pick(condition):
    return jnp.where(condition, jnp.float32(1.0), jnp.float32(0.0))


def row_coefficients(maps, child, quarter):
    entries = [maps[child, quarter, t] for t in range(7)]
    same = [pick(entries[p] == p) if p < 7 else None for p in range(8)]
    above = [pick(entries[p - 1] == p) if p > 0 else None for p in range(8)]
    return same, above


def place(same, above, p, blocks):
    if p == 0:
        return blocks(0) * same[0]
    if p == 7:
        return blocks(6) * above[7]
    return blocks(p) * same[p] + blocks(p - 1) * above[p]


def kernel(
    update, own, maps, out,
    mine, theirs, own_mine, own_theirs, tile1, s1, a1, v_mine, v_theirs, z, x, u, head_mine, head_theirs, tile2, s2, a2,
    local, ex_s, ex_r, f1_s, f1_r, b1_s, b1_r, a1_s, a1_r, zx_s, zx_r, f2_s, f2_r, a2_s, a2_r,
):
    leaf, r, c = lax.axis_index("leaf"), lax.axis_index("frow"), lax.axis_index("fcol")
    twin = leaf + 1 - 2 * lax.rem(leaf, 2)
    pair = leaf // 2
    other = pair + 1 - 2 * lax.rem(pair, 2)
    far = other * 2 + lax.rem(leaf, 2)
    rc, cc = pl.multiple_of(r * 128, 128), pl.multiple_of(c * 128, 128)

    loads = [
        pltpu.make_async_copy(update.at[pl.ds(0, 128), pl.ds(0, 256)], mine.at[pl.ds(0, 128)], local.at[0]),
        pltpu.make_async_copy(own, own_mine, local.at[1]),
        pltpu.make_async_copy(update.at[pl.ds(128, 768), pl.ds(0, 256)], mine.at[pl.ds(128, 768)], local.at[2]),
    ]
    for copy in loads:
        copy.start()

    def send(src, dst, s, t, to):
        copy = pltpu.make_async_remote_copy(
            src_ref=src, dst_ref=dst, send_sem=s, recv_sem=t, device_id=to, device_id_type=MESH
        )
        return copy

    plane = [(i, j) for i in range(4) for j in range(4) if (i, j) != (0, 0)]

    def at(i, j):
        return {"frow": lax.rem(r + i, 4), "fcol": lax.rem(c + j, 4)}

    barrier = pltpu.get_barrier_semaphore()
    pl.semaphore_signal(barrier, inc=1, device_id={"leaf": twin}, device_id_type=MESH)
    pl.semaphore_signal(barrier, inc=1, device_id={"leaf": far}, device_id_type=MESH)
    for i, j in plane:
        pl.semaphore_signal(barrier, inc=1, device_id=at(i, j), device_id_type=MESH)
    pl.semaphore_wait(barrier, 17)

    swaps = [
        send(update.at[pl.ds(0, 128), pl.ds(0, 256)], theirs.at[pl.ds(0, 128)], ex_s.at[0], ex_r.at[0], {"leaf": twin}),
        send(own, own_theirs, ex_s.at[1], ex_r.at[1], {"leaf": twin}),
        send(update.at[pl.ds(128, 768), pl.ds(0, 256)], theirs.at[pl.ds(128, 768)], ex_s.at[2], ex_r.at[2], {"leaf": twin}),
    ]
    for copy in swaps:
        copy.start()

    sides = []
    for ref, child in ((mine, leaf), (theirs, twin)):
        same, above = row_coefficients(maps, child, r)
        first, second = maps[child, c, 0], maps[child, c, 1]
        sides.append((ref, same, above, pick(first == 0), pick(first == 1), pick(second == 1)))

    def front1(p, column):
        total = None
        for ref, same, above, zero, one, two in sides:
            def blocks(t):
                left = ref[128 * t:128 * t + 128, 0:128]
                if column == 0:
                    return left * zero
                return left * one + ref[128 * t:128 * t + 128, 128:256] * two
            part = place(same, above, p, blocks)
            total = part if total is None else total + part
        return total

    loads[0].wait()
    loads[1].wait()
    swaps[0].wait_recv()
    swaps[1].wait_recv()
    pivot = front1(0, 0) + (own_mine[0] + own_theirs[0])
    side = front1(0, 1)
    tile1[0] = pivot
    tile1[1] = side
    s1[r, :, pl.ds(cc, 128)] = pivot
    s1[r, :, 512:640] = side

    def spread(tile, store, s, t):
        return [send(tile, store.at[r, :, pl.ds(cc, 128)], s.at[4 * i + j], t.at[4 * i + j], at(i, j)) for i, j in plane]

    def gather(tile, store, s, t):
        copies = []
        for i, j in plane:
            fr, fc = lax.rem(r + 4 - i, 4), lax.rem(c + 4 - j, 4)
            place_ = store.at[fr, :, pl.ds(pl.multiple_of(fc * 128, 128), 128)]
            copies.append(send(tile, place_, s.at[4 * i + j], t.at[4 * i + j], at(i, j)))
        return copies

    def rows_out(a, s, t):
        block = a.at[:, pl.ds(cc, 128)]
        return [send(block, block, s.at[j], t.at[j], at(0, j)) for j in range(1, 4)]

    def rows_in(a, s, t):
        copies = []
        for j in range(1, 4):
            fc = pl.multiple_of(lax.rem(c + 4 - j, 4) * 128, 128)
            block = a.at[:, pl.ds(fc, 128)]
            copies.append(send(block, block, s.at[j], t.at[j], at(0, j)))
        return copies

    out1 = spread(tile1.at[0], s1, f1_s, f1_r)
    side1 = [send(tile1.at[1], s1.at[r, :, pl.ds(512, 128)], b1_s.at[i], b1_r.at[i], at(i, 0)) for i in range(1, 4)]
    for copy in out1 + side1:
        copy.start()

    loads[2].wait()
    swaps[2].wait_recv()
    for p in range(1, 8):
        a1[128 * (p - 1):128 * p, pl.ds(cc, 128)] = front1(p, 0)
    rows1 = rows_out(a1, a1_s, a1_r)
    for copy in rows1:
        copy.start()
    for p in range(1, 8):
        v_mine[128 * (p - 1):128 * p, :] = front1(p, 1)

    for copy in gather(tile1.at[0], s1, f1_s, f1_r):
        copy.wait_recv()
    for i in range(1, 4):
        send(
            tile1.at[1], s1.at[lax.rem(r + 4 - i, 4), :, pl.ds(512, 128)], b1_s.at[i], b1_r.at[i], at(i, 0)
        ).wait_recv()
    block_factor(s1, x, None, 640, z)
    for copy in rows_in(a1, a1_s, a1_r):
        copy.wait_recv()

    sides2 = []
    for child, ref in ((32 + pair, v_mine), (32 + other, v_theirs)):
        same, above = row_coefficients(maps, child, r)
        sides2.append((ref, same, above, pick(maps[child, c, 0] == 0)))

    v_mine[0:128, :] = v_mine[0:128, :] - mm(a1[0:128, :], z[...], 1, 0)
    _, same, _, zero = sides2[0]
    head_mine[...] = v_mine[0:128, :] * same[0] * zero + (own_mine[1] + own_theirs[1])
    head = send(head_mine, head_theirs, zx_s.at[0], zx_r.at[0], {"leaf": far})
    head.start()
    for lo in range(128, 896, 256):
        v_mine[lo:lo + 256, :] = v_mine[lo:lo + 256, :] - mm(a1[lo:lo + 256, :], z[...], 1, 0)
    rest = send(v_mine, v_theirs, zx_s.at[1], zx_r.at[1], {"leaf": far})
    rest.start()

    head.wait_recv()
    pivot = head_mine[...] + head_theirs[...]
    tile2[...] = pivot
    s2[r, :, pl.ds(cc, 128)] = pivot
    out2 = spread(tile2, s2, f2_s, f2_r)
    for copy in out2:
        copy.start()
    rest.wait_recv()
    for p in range(1, 8):
        total = None
        for ref, same, above, zero in sides2:
            part = place(same, above, p, lambda t: ref[128 * t:128 * t + 128, :]) * zero
            total = part if total is None else total + part
        a2[128 * (p - 1):128 * p, pl.ds(cc, 128)] = total
    rows2 = rows_out(a2, a2_s, a2_r)
    for copy in rows2:
        copy.start()
    for copy in gather(tile2, s2, f2_s, f2_r):
        copy.wait_recv()
    block_factor(s2, x, u, 512)
    for copy in rows_in(a2, a2_s, a2_r):
        copy.wait_recv()

    below = s2[c, :, pl.ds(rc, 128)] * pick(r > c) + u[c] * pick(r == c)
    out[0:128, :] = below.T
    lanes = lax.broadcasted_iota(jnp.int32, (128, 512), 1)
    inverse = jnp.where(lanes < (c + 1) * 128, s2[c], 0.0)
    for lo in range(0, 896, 128):
        out[128 + lo:256 + lo, :] = mm(a2[lo:lo + 128, :], inverse, 1, 1)
    for copy in swaps + out1 + side1 + rows1 + [head, rest] + out2 + rows2:
        copy.wait_send()


def on_device(child_update, own_part, child_maps):
    shapes = [
        (896, 256), (896, 256), (2, 128, 128), (2, 128, 128), (2, 128, 128), (4, 128, 640), (896, 512), (896, 128), (896, 128),
        (512, 128), (128, 128), (4, 128, 128), (128, 128), (128, 128), (128, 128), (4, 128, 512), (896, 512),
    ]
    sems = [3, 3, 3, 16, 16, 4, 4, 4, 4, 2, 2, 16, 16, 4, 4]
    panel = pl.pallas_call(
        kernel,
        out_shape=jax.ShapeDtypeStruct((1024, 128), jnp.float32),
        in_specs=[
            pl.BlockSpec(memory_space=pl.ANY),
            pl.BlockSpec(memory_space=pl.ANY),
            pl.BlockSpec(memory_space=pltpu.SMEM),
        ],
        out_specs=pl.BlockSpec(memory_space=pltpu.VMEM),
        scratch_shapes=[pltpu.VMEM(s, jnp.float32) for s in shapes] + [pltpu.SemaphoreType.DMA((n,)) for n in sems],
        compiler_params=pltpu.CompilerParams(collective_id=0, has_side_effects=True, vmem_limit_bytes=48 << 20),
        name="merge",
    )(child_update[0], own_part[0], child_maps)
    return panel[None]


def solution(mesh):
    in_specs = (P("leaf", "frow", "fcol"), P("leaf", None, "frow", "fcol"), P())
    out_specs = P("leaf", "frow", "fcol")
    return jax.shard_map(on_device, mesh=mesh, in_specs=in_specs, out_specs=out_specs, check_vma=False)
```

```python
import jax
import jax.numpy as jnp
from jax import lax
from jax.experimental import pallas as pl
from jax.experimental.pallas import tpu as pltpu
from jax.sharding import PartitionSpec as P

HI = lax.Precision.HIGHEST
MESH = pl.DeviceIdType.MESH
HALF = 64


def mm(a, b, ca, cb):
    return lax.dot_general(a, b, (((ca,), (cb,)), ((), ())), precision=HI, preferred_element_type=jnp.float32)


def spread_column(v, j):
    return jnp.broadcast_to(v[:, j:j + 1], (8, 128))


def spread_row(v, j):
    return jnp.broadcast_to(v[j:j + 1, :], (8, 128))


def tree(terms):
    while len(terms) > 1:
        terms = [terms[i] + terms[i + 1] if i + 1 < len(terms) else terms[i] for i in range(0, len(terms), 2)]
    return terms[0]


def diag_factor(rows, zero, x_ref, middle):
    lane = lax.broadcasted_iota(jnp.int32, (8, 128), 1)
    sub = lax.broadcasted_iota(jnp.int32, (8, 128), 0)
    c = [spread_column(rows[0], j) + zero for j in range(8)]
    for s in range(16):
        if s == 8:
            middle()
        base = 8 * s
        here = (lane >= base) & (lane < base + 8)
        more = s < 15
        a = {(i, j): spread_row(c[j], i) for j in range(8) for i in range(j, 8)}
        unit = jnp.where(here, (lane - base == sub).astype(jnp.float32), rows[s])
        w = [spread_row(unit, j) for j in range(8)]
        if more:
            y = [spread_column(rows[s + 1], base + j) for j in range(8)]
            d = [spread_column(rows[s + 1], base + 8 + j) for j in range(8)]
        low, inv = {}, {}
        for j in range(8):
            inv[j] = lax.rsqrt(a[j, j])
            for i in range(j + 1, 8):
                low[i, j] = a[i, j] * inv[j]
            for k in range(j + 1, 8):
                for i in range(k, 8):
                    a[i, k] = a[i, k] - low[i, j] * low[k, j]
            w[j] = w[j] * inv[j]
            for k in range(j + 1, 8):
                w[k] = w[k] - low[k, j] * w[j]
            if more:
                y[j] = y[j] * inv[j]
                for k in range(j + 1, 8):
                    y[k] = y[k] - low[k, j] * y[j]
                for k in range(8):
                    d[k] = d[k] - y[j] * spread_row(y[j], k)
        if more:
            c = d
            rows[s + 1] = jnp.where(here, 0.0, rows[s + 1]) - tree([y[j] * w[j] for j in range(8)])
            g = list(w)
            for j in range(7, -1, -1):
                g[j] = g[j] * inv[j]
                for k in range(j):
                    g[k] = g[k] - low[j, k] * g[j]
            for i in range(s + 2, 16):
                part = tree([spread_column(rows[i], base + j) * g[j] for j in range(8)])
                rows[i] = jnp.where(here, 0.0, rows[i]) - part
        done = w[7]
        for i in range(6, -1, -1):
            done = jnp.where(sub <= i, w[i], done)
        x_ref[base:base + 8, :] = jnp.where(lane < base + 8, done, 0.0)


def block_factor(s_ref, x_ref, u_ref, z_ref, zero_ref, before, middle, after):
    def step(j, _):
        cj = pl.multiple_of(j * 128, 128)
        before(j)
        zero = zero_ref[...]
        rows = [s_ref[j, 8 * i:8 * i + 8, pl.ds(cj, 128)] for i in range(16)]
        if u_ref is not None:
            u_ref[j] = s_ref[j, :, pl.ds(cj, 128)]
        diag_factor(rows, zero, x_ref, lambda: middle(j))
        after(j)
        r_i = lax.broadcasted_iota(jnp.int32, (128, 128), 0)
        c_i = lax.broadcasted_iota(jnp.int32, (128, 128), 1)
        s_ref[j, :, pl.ds(cj, 128)] = (r_i == c_i).astype(jnp.float32)
        s_ref[j] = mm(x_ref[...], s_ref[j], 1, 0)

        def trail(i, _):
            ci = pl.multiple_of(i * 128, 128)
            s_ref[i, :, pl.ds(cj, 128)] = jnp.zeros((128, 128), jnp.float32)
            s_ref[i] = s_ref[i] - mm(s_ref[j, :, pl.ds(ci, 128)], s_ref[j], 0, 0)
            return 0

        lax.fori_loop(j + 1, 4, trail, 0)
        if z_ref is not None:
            lanes = lax.broadcasted_iota(jnp.int32, (128, 512), 1)
            inverse = jnp.where(lanes < (j + 1) * 128, s_ref[j, :, 0:512], 0.0)
            z_ref[...] += mm(inverse, s_ref[j, :, 512:640], 0, 0)
        return 0

    if z_ref is not None:
        z_ref[...] = jnp.zeros_like(z_ref)
    lax.fori_loop(0, 4, step, 0)


def pick(condition):
    return jnp.where(condition, jnp.float32(1.0), jnp.float32(0.0))


def row_coefficients(maps, child, quarter):
    entries = [maps[t, quarter, child] for t in range(7)]
    same = [pick(entries[p] == p) if p < 7 else None for p in range(8)]
    above = [pick(entries[p - 1] == p) if p > 0 else None for p in range(8)]
    return same, above


def place(same, above, p, blocks):
    if p == 0:
        return blocks(0) * same[0]
    if p == 7:
        return blocks(6) * above[7]
    return blocks(p) * same[p] + blocks(p - 1) * above[p]


def kernel(
    update, own, maps, out,
    mine, theirs, own_mine, own_theirs, tile1, s1, a1, v_mine, v_theirs, z, x, u, head_mine, head_theirs, tile2, s2, a2, zero,
    local, ex_s, ex_r, b1_s, b1_r, zx_s, zx_r, f1_s, f1_r, w1_s, w1_r, a1_s, a1_r, f2_s, f2_r, w2_s, w2_r, a2_s, a2_r, t_s, t_r,
):
    leaf, r, c = lax.axis_index("leaf"), lax.axis_index("frow"), lax.axis_index("fcol")
    core = lax.rem(leaf, 2)
    twin = leaf + 1 - 2 * core
    pair = leaf // 2
    other = pair + 1 - 2 * lax.rem(pair, 2)
    far = other * 2 + core
    cc, rc = pl.multiple_of(c * 128, 128), pl.multiple_of(r * 128, 128)
    h, g = pl.multiple_of(core * HALF, HALF), pl.multiple_of(HALF - core * HALF, HALF)
    upper = r <= c
    plane = [(i, j) for i in range(4) for j in range(4) if (i, j) != (0, 0)]

    def at(i, j):
        return {"frow": lax.rem(r + i, 4), "fcol": lax.rem(c + j, 4)}

    def send(src, dst, s, t, to):
        return pltpu.make_async_remote_copy(
            src_ref=src, dst_ref=dst, send_sem=s, recv_sem=t, device_id=to, device_id_type=MESH
        )

    loads = [
        pltpu.make_async_copy(update.at[pl.ds(0, 1), pl.ds(h, HALF), pl.ds(0, 256)], mine.at[pl.ds(0, 1)], local.at[0]),
        pltpu.make_async_copy(own.at[:, pl.ds(h, HALF), :], own_mine, local.at[1]),
        pltpu.make_async_copy(update.at[pl.ds(1, 6), pl.ds(h, HALF), pl.ds(0, 256)], mine.at[pl.ds(1, 6)], local.at[2]),
    ]
    for copy in loads:
        copy.start()

    barrier = pltpu.get_barrier_semaphore()
    pl.semaphore_signal(barrier, inc=1, device_id={"leaf": twin}, device_id_type=MESH)
    for i, j in plane:
        pl.semaphore_signal(barrier, inc=1, device_id=at(i, j), device_id_type=MESH)
    pl.semaphore_signal(barrier, inc=1, device_id={"leaf": far}, device_id_type=MESH)
    zero[...] = jnp.zeros_like(zero)
    pl.semaphore_wait(barrier, 17)

    swaps = [
        send(
            update.at[pl.ds(0, 1), pl.ds(g, HALF), pl.ds(0, 256)], theirs.at[pl.ds(0, 1)],
            ex_s.at[0], ex_r.at[0], {"leaf": twin},
        ),
        send(own.at[:, pl.ds(g, HALF), :], own_theirs, ex_s.at[1], ex_r.at[1], {"leaf": twin}),
        send(
            update.at[pl.ds(1, 6), pl.ds(g, HALF), pl.ds(0, 256)], theirs.at[pl.ds(1, 6)],
            ex_s.at[2], ex_r.at[2], {"leaf": twin},
        ),
    ]
    for copy in swaps:
        copy.start()

    sides = []
    for ref, child in ((mine, leaf), (theirs, twin)):
        same, above = row_coefficients(maps, child, r)
        first, second = maps[0, c, child], maps[1, c, child]
        sides.append((ref, same, above, pick(first == 0), pick(first == 1), pick(second == 1)))

    def front1(p, column):
        total = None
        for ref, same, above, none, one, two in sides:

            def blocks(t):
                left = ref[t, :, 0:128]
                if column == 0:
                    return left * none
                return left * one + ref[t, :, 128:256] * two

            part = place(same, above, p, blocks)
            total = part if total is None else total + part
        return total

    def spread(tile, store, s, t):
        return [
            send(tile, store.at[r, pl.ds(h, HALF), pl.ds(cc, 128)], s.at[4 * i + j], t.at[4 * r + c], at(i, j))
            for i, j in plane
        ]

    def start_spread(copies):
        @pl.when(upper)
        def _():
            for copy in copies:
                copy.start()

    def finish_spread(copies):
        @pl.when(upper)
        def _():
            for copy in copies:
                copy.wait_send()

    def arrived(tile, store, s, t, i, j):
        @pl.when(jnp.logical_or(r != i, c != j))
        def _():
            send(
                tile, store.at[i, pl.ds(h, HALF), pl.ds(128 * j, 128)], s.at[4 * i + j], t.at[4 * i + j], at(0, 1)
            ).wait_recv()

    def twin_parts(store, s, t, width, offset):
        bounds = [(0, 0, 128), (0, 128, width), (1, 128, width), (2, 256, width), (3, 384, width)]
        copies = []
        for n, (i, lo, hi) in enumerate(bounds):
            part = store.at[i, pl.ds(offset, HALF), pl.ds(lo, hi - lo)]
            copies.append(send(part, part, s.at[n], t.at[n], {"leaf": twin}))
        return copies

    def rows_out(store, s, t):
        block = store.at[:, pl.ds(cc, 128)]
        return [send(block, block, s.at[j], t.at[j], at(0, j)) for j in range(1, 4)]

    def rows_in(store, s, t):
        copies = []
        for j in range(1, 4):
            block = store.at[:, pl.ds(pl.multiple_of(lax.rem(c + 4 - j, 4) * 128, 128), 128)]
            copies.append(send(block, block, s.at[j], t.at[j], at(0, j)))
        return copies

    loads[0].wait()
    loads[1].wait()
    swaps[0].wait_recv()
    swaps[1].wait_recv()
    pivot = front1(0, 0) + (own_mine[0] + own_theirs[0])
    tile1[0] = pivot
    out1 = spread(tile1.at[0], s1, f1_s, f1_r)
    start_spread(out1)
    s1[r, pl.ds(h, HALF), pl.ds(cc, 128)] = pivot
    side = front1(0, 1)
    tile1[1] = side
    side1 = [
        send(tile1.at[1], s1.at[r, pl.ds(h, HALF), pl.ds(512, 128)], b1_s.at[i], b1_r.at[i], at(i, 0)) for i in range(1, 4)
    ]
    for copy in side1:
        copy.start()
    s1[r, pl.ds(h, HALF), pl.ds(512, 128)] = side

    loads[2].wait()
    swaps[2].wait_recv()
    for p in range(1, 8):
        a1[HALF * (p - 1):HALF * p, pl.ds(cc, 128)] = front1(p, 0)
        v_mine[HALF * (p - 1):HALF * p, :] = front1(p, 1)
    rows1 = rows_out(a1, a1_s, a1_r)

    def begin(tile, store, s, t, parts):
        arrived(tile, store, s, t, 0, 0)
        give, take = parts
        give[0].start()
        take[0].wait_recv()

    def middle_of(tile, store, s, t, parts, rest):
        def middle(j):
            @pl.when(j == 0)
            def _():
                for i in range(4):
                    for k in range(max(i, 1), 4):
                        arrived(tile, store, s, t, i, k)
                rest()
                for copy in parts[0][1:]:
                    copy.start()

        return middle

    def after_of(parts):
        def after(j):
            @pl.when(j == 0)
            def _():
                for copy in parts[1][1:]:
                    copy.wait_recv()
                for copy in parts[0]:
                    copy.wait_send()

        return after

    def nothing(j):
        return None

    def side_in_rows_out():
        for i in range(1, 4):
            send(
                tile1.at[1], s1.at[lax.rem(r + 4 - i, 4), pl.ds(h, HALF), pl.ds(512, 128)], b1_s.at[i], b1_r.at[i], at(i, 0)
            ).wait_recv()
        for copy in rows1:
            copy.start()

    parts1 = twin_parts(s1, w1_s, w1_r, 640, h), twin_parts(s1, w1_s, w1_r, 640, g)
    begin(tile1.at[0], s1, f1_s, f1_r, parts1)
    block_factor(
        s1, x, None, z, zero, nothing, middle_of(tile1.at[0], s1, f1_s, f1_r, parts1, side_in_rows_out), after_of(parts1)
    )
    for copy in rows_in(a1, a1_s, a1_r):
        copy.wait_recv()

    sides2 = []
    for child, ref in ((32 + pair, v_mine), (32 + other, v_theirs)):
        same, above = row_coefficients(maps, child, r)
        sides2.append((ref, same, above, pick(maps[0, c, child] == 0)))

    v_mine[0:HALF, :] = v_mine[0:HALF, :] - mm(a1[0:HALF, :], z[...], 1, 0)
    _, same, _, first = sides2[0]
    head_mine[...] = v_mine[0:HALF, :] * same[0] * first + (own_mine[1] + own_theirs[1])
    head = send(head_mine, head_theirs, zx_s.at[0], zx_r.at[0], {"leaf": far})
    head.start()
    v_mine[HALF:, :] = v_mine[HALF:, :] - mm(a1[HALF:, :], z[...], 1, 0)
    rest = send(v_mine, v_theirs, zx_s.at[1], zx_r.at[1], {"leaf": far})
    rest.start()

    head.wait_recv()
    pivot = head_mine[...] + head_theirs[...]
    tile2[...] = pivot
    out2 = spread(tile2, s2, f2_s, f2_r)
    start_spread(out2)
    s2[r, pl.ds(h, HALF), pl.ds(cc, 128)] = pivot
    rest.wait_recv()
    a2_own = a2.at[core]
    for p in range(1, 8):
        total = None
        for ref, same, above, first in sides2:
            part = place(same, above, p, lambda t: ref[HALF * t:HALF * t + HALF, :]) * first
            total = part if total is None else total + part
        a2[core, HALF * (p - 1):HALF * p, pl.ds(cc, 128)] = total
    rows2 = rows_out(a2_own, a2_s, a2_r)

    def rows_out2():
        for copy in rows2:
            copy.start()

    a2_give = send(a2_own, a2_own, t_s.at[0], t_r.at[0], {"leaf": twin})
    a2_twin = a2.at[1 - core]
    a2_take = send(a2_twin, a2_twin, t_s.at[0], t_r.at[0], {"leaf": twin})

    def before2(j):
        @pl.when(j == 3)
        def _():
            for copy in rows_in(a2_own, a2_s, a2_r):
                copy.wait_recv()
            a2_give.start()

    parts2 = twin_parts(s2, w2_s, w2_r, 512, h), twin_parts(s2, w2_s, w2_r, 512, g)
    begin(tile2, s2, f2_s, f2_r, parts2)
    block_factor(s2, x, u, None, zero, before2, middle_of(tile2, s2, f2_s, f2_r, parts2, rows_out2), after_of(parts2))

    lanes = lax.broadcasted_iota(jnp.int32, (128, 512), 1)
    inverse = jnp.where(lanes < (c + 1) * 128, s2[c], 0.0)

    def lower_rows(k):
        result = mm(a2[k], inverse, 1, 1)
        k0 = pl.multiple_of(k * HALF, HALF)
        for p in range(7):
            out[p + 1, pl.ds(k0, HALF), :] = result[HALF * p:HALF * p + HALF, :]

    lower_rows(core)
    r_i = lax.broadcasted_iota(jnp.int32, (128, 128), 0)
    c_i = lax.broadcasted_iota(jnp.int32, (128, 128), 1)
    corner = jnp.where(r_i >= c_i, mm(u[c], s2[c, :, pl.ds(cc, 128)], 1, 1), 0.0)
    out[0] = s2[c, :, pl.ds(rc, 128)].T * pick(r > c) + corner * pick(r == c)
    a2_take.wait_recv()
    lower_rows(1 - core)
    a2_give.wait_send()
    for copy in swaps + side1 + rows1 + [head, rest] + rows2:
        copy.wait_send()
    finish_spread(out1)
    finish_spread(out2)


def on_device(child_update, own_part, child_maps):
    shapes = [
        (7, 64, 256), (7, 64, 256), (2, 64, 128), (2, 64, 128), (2, 64, 128), (4, 128, 640), (448, 512), (448, 128), (448, 128),
        (512, 128), (128, 128), (4, 128, 128), (64, 128), (64, 128), (64, 128), (4, 128, 512), (2, 448, 512), (8, 128),
    ]
    sems = [3, 3, 3, 4, 4, 2, 2] + [16, 16, 5, 5, 4, 4] * 2 + [1, 1]
    panel = pl.pallas_call(
        kernel,
        out_shape=jax.ShapeDtypeStruct((8, 128, 128), jnp.float32),
        in_specs=[
            pl.BlockSpec(memory_space=pl.ANY),
            pl.BlockSpec(memory_space=pl.ANY),
            pl.BlockSpec(memory_space=pltpu.SMEM),
        ],
        out_specs=pl.BlockSpec(memory_space=pltpu.VMEM),
        scratch_shapes=[pltpu.VMEM(s, jnp.float32) for s in shapes] + [pltpu.SemaphoreType.DMA((n,)) for n in sems],
        compiler_params=pltpu.CompilerParams(collective_id=0, has_side_effects=True, vmem_limit_bytes=62 << 20),
        name="merge",
    )(child_update[0].reshape(7, 128, 896), own_part[0], child_maps.transpose(2, 1, 0))
    return panel.reshape(1, 1024, 128)


def solution(mesh):
    in_specs = (P("leaf", "frow", "fcol"), P("leaf", None, "frow", "fcol"), P())
    out_specs = P("leaf", "frow", "fcol")
    return jax.shard_map(on_device, mesh=mesh, in_specs=in_specs, out_specs=out_specs, check_vma=False)
```

```python
import jax
import jax.numpy as jnp
from jax import lax
from jax.experimental import pallas as pl
from jax.experimental.pallas import tpu as pltpu
from jax.sharding import PartitionSpec as P

MESH = pl.DeviceIdType.MESH
HALF = 64


def thirds(v):
    high = v.astype(jnp.bfloat16)
    rest = v - high.astype(jnp.float32)
    middle = rest.astype(jnp.bfloat16)
    return high, middle, (rest - middle.astype(jnp.float32)).astype(jnp.bfloat16)


def left(v):
    h, m, l = thirds(v)
    return jnp.concatenate([h, h, m, h, m, l], 1)


def right(v):
    h, m, l = thirds(v)
    return jnp.concatenate([h, m, h, l, m, h], 0)


def dot(a, b):
    return lax.dot_general(a, b, (((1,), (0,)), ((), ())), preferred_element_type=jnp.float32)


def spread_column(v, j):
    return jnp.broadcast_to(v[:, j:j + 1], (8, 128))


def spread_row(v, j):
    return jnp.broadcast_to(v[j:j + 1, :], (8, 128))


def tree(terms):
    while len(terms) > 1:
        terms = [terms[i] + terms[i + 1] if i + 1 < len(terms) else terms[i] for i in range(0, len(terms), 2)]
    return terms[0]


def diag_factor(rows, zero, x_ref, middle):
    lane = lax.broadcasted_iota(jnp.int32, (8, 128), 1)
    sub = lax.broadcasted_iota(jnp.int32, (8, 128), 0)
    c = [spread_column(rows[0], j) + zero for j in range(8)]
    for s in range(16):
        if s == 8:
            middle()
        base = 8 * s
        here = (lane >= base) & (lane < base + 8)
        more = s < 15
        a = {(i, j): spread_row(c[j], i) for j in range(8) for i in range(j, 8)}
        unit = jnp.where(here, (lane - base == sub).astype(jnp.float32), rows[s])
        w = [spread_row(unit, j) for j in range(8)]
        if more:
            y = [spread_column(rows[s + 1], base + j) for j in range(8)]
            d = [spread_column(rows[s + 1], base + 8 + j) for j in range(8)]
        low, inv = {}, {}
        for j in range(8):
            inv[j] = lax.rsqrt(a[j, j])
            for i in range(j + 1, 8):
                low[i, j] = a[i, j] * inv[j]
            for k in range(j + 1, 8):
                for i in range(k, 8):
                    a[i, k] = a[i, k] - low[i, j] * low[k, j]
            w[j] = w[j] * inv[j]
            for k in range(j + 1, 8):
                w[k] = w[k] - low[k, j] * w[j]
            if more:
                y[j] = y[j] * inv[j]
                for k in range(j + 1, 8):
                    y[k] = y[k] - low[k, j] * y[j]
                for k in range(8):
                    d[k] = d[k] - y[j] * spread_row(y[j], k)
        if more:
            c = d
            rows[s + 1] = jnp.where(here, 0.0, rows[s + 1]) - tree([y[j] * w[j] for j in range(8)])
            g = list(w)
            for j in range(7, -1, -1):
                g[j] = g[j] * inv[j]
                for k in range(j):
                    g[k] = g[k] - low[j, k] * g[j]
            for i in range(s + 2, 16):
                part = tree([spread_column(rows[i], base + j) * g[j] for j in range(8)])
                rows[i] = jnp.where(here, 0.0, rows[i]) - part
        done = w[7]
        for i in range(6, -1, -1):
            done = jnp.where(sub <= i, w[i], done)
        x_ref[base:base + 8, :] = jnp.where(lane < base + 8, done, 0.0)


def block_factor(s_ref, x_ref, u_ref, z_ref, zero_ref, before, middle, after, later):
    def step(j, _):
        cj = pl.multiple_of(j * 128, 128)
        before(j)
        zero = zero_ref[...]
        rows = [s_ref[j, 8 * i:8 * i + 8, pl.ds(cj, 128)] for i in range(16)]
        if u_ref is not None:
            u_ref[j] = s_ref[j, :, pl.ds(cj, 128)]
        diag_factor(rows, zero, x_ref, lambda: middle(j))
        after(j)
        r_i = lax.broadcasted_iota(jnp.int32, (128, 128), 0)
        c_i = lax.broadcasted_iota(jnp.int32, (128, 128), 1)
        s_ref[j, :, pl.ds(cj, 128)] = (r_i == c_i).astype(jnp.float32)
        u = dot(left(x_ref[...]), right(s_ref[j]))
        s_ref[j] = u
        later(j)
        u = right(u)

        def trail(i, _):
            ci = pl.multiple_of(i * 128, 128)
            s_ref[i, :, pl.ds(cj, 128)] = jnp.zeros((128, 128), jnp.float32)
            s_ref[i] = s_ref[i] - dot(left(s_ref[j, :, pl.ds(ci, 128)].T), u)
            return 0

        lax.fori_loop(j + 1, 4, trail, 0)
        if z_ref is not None:
            lanes = lax.broadcasted_iota(jnp.int32, (128, 512), 1)
            inverse = jnp.where(lanes < (j + 1) * 128, s_ref[j, :, 0:512], 0.0)
            z_ref[...] += dot(left(inverse.T), u[:, 512:640])
        return 0

    if z_ref is not None:
        z_ref[...] = jnp.zeros_like(z_ref)
    lax.fori_loop(0, 4, step, 0)


def pick(condition):
    return jnp.where(condition, jnp.float32(1.0), jnp.float32(0.0))


def row_coefficients(maps, child, quarter):
    entries = [maps[t, quarter, child] for t in range(7)]
    same = [pick(entries[p] == p) if p < 7 else None for p in range(8)]
    above = [pick(entries[p - 1] == p) if p > 0 else None for p in range(8)]
    return same, above


def place(same, above, p, blocks):
    if p == 0:
        return blocks(0) * same[0]
    if p == 7:
        return blocks(6) * above[7]
    return blocks(p) * same[p] + blocks(p - 1) * above[p]


def kernel(
    update, own, maps_in, out,
    mine, theirs, own_mine, own_theirs, tile1, s1, a1, v_mine, v_theirs, z, x, u, head_mine, head_theirs, tile2, s2, a2, zero, maps,
    local, ex_s, ex_r, b1_s, b1_r, zx_s, zx_r, f1_s, f1_r, w1_s, w1_r, a1_s, a1_r, f2_s, f2_r, w2_s, w2_r, a2_s, a2_r, t_s, t_r,
):
    leaf, r, c = lax.axis_index("leaf"), lax.axis_index("frow"), lax.axis_index("fcol")
    core = lax.rem(leaf, 2)
    twin = leaf + 1 - 2 * core
    pair = leaf // 2
    other = pair + 1 - 2 * lax.rem(pair, 2)
    far = other * 2 + core
    cc, rc = pl.multiple_of(c * 128, 128), pl.multiple_of(r * 128, 128)
    h, g = pl.multiple_of(core * HALF, HALF), pl.multiple_of(HALF - core * HALF, HALF)
    upper = jnp.logical_or(jnp.logical_and(r <= c, c - r < 3), r - c == 3)
    plane = [(i, j) for i in range(4) for j in range(4) if (i, j) != (0, 0)]

    def at(i, j):
        return {"frow": lax.rem(r + i, 4), "fcol": lax.rem(c + j, 4)}

    def send(src, dst, s, t, to):
        return pltpu.make_async_remote_copy(
            src_ref=src, dst_ref=dst, send_sem=s, recv_sem=t, device_id=to, device_id_type=MESH
        )

    loads = [
        pltpu.make_async_copy(update.at[pl.ds(0, 1), pl.ds(h, HALF), pl.ds(0, 256)], mine.at[pl.ds(0, 1)], local.at[0]),
        pltpu.make_async_copy(own.at[:, pl.ds(h, HALF), :], own_mine, local.at[1]),
        pltpu.make_async_copy(maps_in, maps, local.at[3]),
        pltpu.make_async_copy(update.at[pl.ds(1, 6), pl.ds(h, HALF), pl.ds(0, 256)], mine.at[pl.ds(1, 6)], local.at[2]),
    ]
    for copy in loads:
        copy.start()

    barrier = pltpu.get_barrier_semaphore()
    pl.semaphore_signal(barrier, inc=1, device_id={"leaf": twin}, device_id_type=MESH)
    for i, j in plane:
        pl.semaphore_signal(barrier, inc=1, device_id=at(i, j), device_id_type=MESH)
    pl.semaphore_signal(barrier, inc=1, device_id={"leaf": far}, device_id_type=MESH)
    zero[...] = jnp.zeros_like(zero)
    pl.semaphore_wait(barrier, 17)

    swaps = [
        send(
            update.at[pl.ds(0, 1), pl.ds(g, HALF), pl.ds(0, 256)], theirs.at[pl.ds(0, 1)],
            ex_s.at[0], ex_r.at[0], {"leaf": twin},
        ),
        send(own.at[:, pl.ds(g, HALF), :], own_theirs, ex_s.at[1], ex_r.at[1], {"leaf": twin}),
        send(
            update.at[pl.ds(1, 6), pl.ds(g, HALF), pl.ds(0, 256)], theirs.at[pl.ds(1, 6)],
            ex_s.at[2], ex_r.at[2], {"leaf": twin},
        ),
    ]
    for copy in swaps:
        copy.start()

    loads[2].wait()
    sides = []
    for ref, child in ((mine, leaf), (theirs, twin)):
        same, above = row_coefficients(maps, child, r)
        first, second = maps[0, c, child], maps[1, c, child]
        sides.append((ref, same, above, pick(first == 0), pick(first == 1), pick(second == 1)))

    def front1(p, column):
        total = None
        for ref, same, above, none, one, two in sides:

            def blocks(t):
                left = ref[t, :, 0:128]
                if column == 0:
                    return left * none
                return left * one + ref[t, :, 128:256] * two

            part = place(same, above, p, blocks)
            total = part if total is None else total + part
        return total

    def spread(tile, store, s, t):
        return [
            send(tile, store.at[r, pl.ds(h, HALF), pl.ds(cc, 128)], s.at[4 * i + j], t.at[4 * r + c], at(i, j))
            for i, j in plane
        ]

    def start_spread(copies):
        @pl.when(upper)
        def _():
            for copy in copies:
                copy.start()

    def finish_spread(copies):
        @pl.when(upper)
        def _():
            for copy in copies:
                copy.wait_send()

    def arrived(tile, store, s, t, i, j):
        @pl.when(jnp.logical_or(r != i, c != j))
        def _():
            send(
                tile, store.at[i, pl.ds(h, HALF), pl.ds(128 * j, 128)], s.at[4 * i + j], t.at[4 * i + j], at(0, 1)
            ).wait_recv()

    def twin_parts(store, s, t, width, offset):
        bounds = [(0, 0, 128), (0, 128, 384), (3, 0, 128), (1, 128, width), (2, 256, width), (3, 384, width)]
        if width > 512:
            bounds.insert(2, (0, 512, width))
        copies = []
        for n, (i, lo, hi) in enumerate(bounds):
            part = store.at[i, pl.ds(offset, HALF), pl.ds(lo, hi - lo)]
            copies.append(send(part, part, s.at[n], t.at[n], {"leaf": twin}))
        return copies

    def rows_out(store, s, t):
        block = store.at[:, pl.ds(cc, 128)]
        return [send(block, block, s.at[j], t.at[j], at(0, j)) for j in range(1, 4)]

    def rows_in(store, s, t):
        copies = []
        for j in range(1, 4):
            block = store.at[:, pl.ds(pl.multiple_of(lax.rem(c + 4 - j, 4) * 128, 128), 128)]
            copies.append(send(block, block, s.at[j], t.at[j], at(0, j)))
        return copies

    loads[0].wait()
    loads[1].wait()
    swaps[0].wait_recv()
    swaps[1].wait_recv()
    pivot = front1(0, 0) + (own_mine[0] + own_theirs[0])
    tile1[0] = pivot
    out1 = spread(tile1.at[0], s1, f1_s, f1_r)
    start_spread(out1)
    s1[r, pl.ds(h, HALF), pl.ds(cc, 128)] = pivot
    side = front1(0, 1)
    tile1[1] = side
    side1 = [
        send(tile1.at[1], s1.at[r, pl.ds(h, HALF), pl.ds(512, 128)], b1_s.at[i], b1_r.at[i], at(i, 0)) for i in range(1, 4)
    ]
    for copy in side1:
        copy.start()
    s1[r, pl.ds(h, HALF), pl.ds(512, 128)] = side

    loads[3].wait()
    swaps[2].wait_recv()
    for p in range(1, 8):
        a1[HALF * (p - 1):HALF * p, pl.ds(cc, 128)] = front1(p, 0)
        v_mine[HALF * (p - 1):HALF * p, :] = front1(p, 1)
    rows1 = rows_out(a1, a1_s, a1_r)

    def begin(tile, store, s, t, parts):
        arrived(tile, store, s, t, 0, 0)
        give, take = parts
        give[0].start()
        take[0].wait_recv()

    def middle_of(tile, store, s, t, parts, rest):
        def middle(j):
            @pl.when(j == 0)
            def _():
                for i, k in ((0, 1), (0, 2), (3, 0), (1, 1), (1, 2), (1, 3), (2, 2), (2, 3), (3, 3)):
                    arrived(tile, store, s, t, i, k)
                rest()
                for copy in parts[0][1:]:
                    copy.start()

        return middle

    def after_of(store, parts):
        head = len(parts[0]) - 3

        def after(j):
            @pl.when(j == 0)
            def _():
                for copy in parts[1][1:head]:
                    copy.wait_recv()
                for copy in parts[0][:head]:
                    copy.wait_send()
                store[0, :, 384:512] = store[3, :, 0:128].T

        def later(j):
            @pl.when(j == 0)
            def _():
                for copy in parts[1][head:]:
                    copy.wait_recv()
                for copy in parts[0][head:]:
                    copy.wait_send()

        return after, later

    def nothing(j):
        return None

    def side_in_rows_out():
        for i in range(1, 4):
            send(
                tile1.at[1], s1.at[lax.rem(r + 4 - i, 4), pl.ds(h, HALF), pl.ds(512, 128)], b1_s.at[i], b1_r.at[i], at(i, 0)
            ).wait_recv()
        for copy in rows1:
            copy.start()

    parts1 = twin_parts(s1, w1_s, w1_r, 640, h), twin_parts(s1, w1_s, w1_r, 640, g)
    begin(tile1.at[0], s1, f1_s, f1_r, parts1)
    block_factor(
        s1, x, None, z, zero, nothing, middle_of(tile1.at[0], s1, f1_s, f1_r, parts1, side_in_rows_out), *after_of(s1, parts1)
    )
    for copy in rows_in(a1, a1_s, a1_r):
        copy.wait_recv()

    sides2 = []
    for child, ref in ((32 + pair, v_mine), (32 + other, v_theirs)):
        same, above = row_coefficients(maps, child, r)
        sides2.append((ref, same, above, pick(maps[0, c, child] == 0)))

    z_right = right(z[...])
    v_mine[0:HALF, :] = v_mine[0:HALF, :] - dot(left(a1[0:HALF, :]), z_right)
    _, same, _, first = sides2[0]
    head_mine[...] = v_mine[0:HALF, :] * same[0] * first + (own_mine[1] + own_theirs[1])
    head = send(head_mine, head_theirs, zx_s.at[0], zx_r.at[0], {"leaf": far})
    head.start()
    v_mine[HALF:, :] = v_mine[HALF:, :] - dot(left(a1[HALF:, :]), z_right)
    rest = send(v_mine, v_theirs, zx_s.at[1], zx_r.at[1], {"leaf": far})
    rest.start()

    head.wait_recv()
    pivot = head_mine[...] + head_theirs[...]
    tile2[...] = pivot
    out2 = spread(tile2, s2, f2_s, f2_r)
    start_spread(out2)
    s2[r, pl.ds(h, HALF), pl.ds(cc, 128)] = pivot
    rest.wait_recv()
    a2_own = a2.at[core]
    for p in range(1, 8):
        total = None
        for ref, same, above, first in sides2:
            part = place(same, above, p, lambda t: ref[HALF * t:HALF * t + HALF, :]) * first
            total = part if total is None else total + part
        a2[core, HALF * (p - 1):HALF * p, pl.ds(cc, 128)] = total
    rows2 = rows_out(a2_own, a2_s, a2_r)

    def rows_out2():
        for copy in rows2:
            copy.start()

    a2_give = send(a2_own, a2_own, t_s.at[0], t_r.at[0], {"leaf": twin})
    a2_twin = a2.at[1 - core]
    a2_take = send(a2_twin, a2_twin, t_s.at[0], t_r.at[0], {"leaf": twin})

    def before2(j):
        @pl.when(j == 3)
        def _():
            for copy in rows_in(a2_own, a2_s, a2_r):
                copy.wait_recv()
            a2_give.start()

    parts2 = twin_parts(s2, w2_s, w2_r, 512, h), twin_parts(s2, w2_s, w2_r, 512, g)
    begin(tile2, s2, f2_s, f2_r, parts2)
    block_factor(s2, x, u, None, zero, before2, middle_of(tile2, s2, f2_s, f2_r, parts2, rows_out2), *after_of(s2, parts2))

    lanes = lax.broadcasted_iota(jnp.int32, (128, 512), 1)
    inverse = right(jnp.where(lanes < (c + 1) * 128, s2[c], 0.0).T)

    def lower_rows(k):
        result = dot(left(a2[k]), inverse)
        k0 = pl.multiple_of(k * HALF, HALF)
        for p in range(7):
            out[p + 1, pl.ds(k0, HALF), :] = result[HALF * p:HALF * p + HALF, :]

    lower_rows(core)
    r_i = lax.broadcasted_iota(jnp.int32, (128, 128), 0)
    c_i = lax.broadcasted_iota(jnp.int32, (128, 128), 1)
    corner = jnp.where(r_i >= c_i, dot(left(u[c]), right(s2[c, :, pl.ds(cc, 128)].T)), 0.0)
    out[0] = s2[c, :, pl.ds(rc, 128)].T * pick(r > c) + corner * pick(r == c)
    a2_take.wait_recv()
    lower_rows(1 - core)
    a2_give.wait_send()
    for copy in swaps + side1 + rows1 + [head, rest] + rows2:
        copy.wait_send()
    finish_spread(out1)
    finish_spread(out2)


def on_device(child_update, own_part, child_maps):
    shapes = [
        (7, 64, 256), (7, 64, 256), (2, 64, 128), (2, 64, 128), (2, 64, 128), (4, 128, 640), (448, 512), (448, 128), (448, 128),
        (512, 128), (128, 128), (4, 128, 128), (64, 128), (64, 128), (64, 128), (4, 128, 512), (2, 448, 512), (8, 128),
    ]
    sems = [4, 3, 3, 4, 4, 2, 2] + [16, 16, 7, 7, 4, 4] * 2 + [1, 1]
    panel = pl.pallas_call(
        kernel,
        out_shape=jax.ShapeDtypeStruct((8, 128, 128), jnp.float32),
        in_specs=[
            pl.BlockSpec(memory_space=pl.ANY),
            pl.BlockSpec(memory_space=pl.ANY),
            pl.BlockSpec(memory_space=pl.ANY),
        ],
        out_specs=pl.BlockSpec(memory_space=pltpu.VMEM),
        scratch_shapes=[pltpu.VMEM(s, jnp.float32) for s in shapes]
        + [pltpu.SMEM((7, 4, 48), jnp.int32)]
        + [pltpu.SemaphoreType.DMA((n,)) for n in sems],
        compiler_params=pltpu.CompilerParams(collective_id=0, has_side_effects=True, vmem_limit_bytes=62 << 20),
        name="merge",
    )(child_update[0].reshape(7, 128, 896), own_part[0], child_maps.transpose(2, 1, 0))
    return panel.reshape(1, 1024, 128)


def solution(mesh):
    in_specs = (P("leaf", "frow", "fcol"), P("leaf", None, "frow", "fcol"), P())
    out_specs = P("leaf", "frow", "fcol")
    return jax.shard_map(on_device, mesh=mesh, in_specs=in_specs, out_specs=out_specs, check_vma=False)
```

```python
import jax
import jax.numpy as jnp
from jax import lax
from jax.experimental import pallas as pl
from jax.experimental.pallas import tpu as pltpu
from jax.sharding import PartitionSpec as P

MESH = pl.DeviceIdType.MESH
HALF = 64


def thirds(v):
    high = v.astype(jnp.bfloat16)
    rest = v - high.astype(jnp.float32)
    middle = rest.astype(jnp.bfloat16)
    return high, middle, (rest - middle.astype(jnp.float32)).astype(jnp.bfloat16)


def left(v):
    h, m, l = thirds(v)
    return jnp.concatenate([h, h, m, h, m, l], 1)


def right(v):
    h, m, l = thirds(v)
    return jnp.concatenate([h, m, h, l, m, h], 0)


def dot(a, b):
    return lax.dot_general(a, b, (((1,), (0,)), ((), ())), preferred_element_type=jnp.float32)


def spread_column(v, j):
    return jnp.broadcast_to(v[:, j:j + 1], (8, 128))


def spread_row(v, j):
    return jnp.broadcast_to(v[j:j + 1, :], (8, 128))


def tree(terms):
    while len(terms) > 1:
        terms = [terms[i] + terms[i + 1] if i + 1 < len(terms) else terms[i] for i in range(0, len(terms), 2)]
    return terms[0]


def diag_factor(rows, zero, x_ref, middle):
    lane = lax.broadcasted_iota(jnp.int32, (8, 128), 1)
    sub = lax.broadcasted_iota(jnp.int32, (8, 128), 0)
    c = [spread_column(rows[0], j) + zero for j in range(8)]
    for s in range(16):
        if s == 8:
            middle()
        base = 8 * s
        here = (lane >= base) & (lane < base + 8)
        more = s < 15
        a = {(i, j): spread_row(c[j], i) for j in range(8) for i in range(j, 8)}
        unit = jnp.where(here, (lane - base == sub).astype(jnp.float32), rows[s])
        w = [spread_row(unit, j) for j in range(8)]
        if more:
            y = [spread_column(rows[s + 1], base + j) for j in range(8)]
            d = [spread_column(rows[s + 1], base + 8 + j) for j in range(8)]
        low, inv = {}, {}
        for j in range(8):
            inv[j] = lax.rsqrt(a[j, j])
            for i in range(j + 1, 8):
                low[i, j] = a[i, j] * inv[j]
            for k in range(j + 1, 8):
                for i in range(k, 8):
                    a[i, k] = a[i, k] - low[i, j] * low[k, j]
            w[j] = w[j] * inv[j]
            for k in range(j + 1, 8):
                w[k] = w[k] - low[k, j] * w[j]
            if more:
                y[j] = y[j] * inv[j]
                for k in range(j + 1, 8):
                    y[k] = y[k] - low[k, j] * y[j]
                for k in range(8):
                    d[k] = d[k] - y[j] * spread_row(y[j], k)
        if more:
            c = d
            rows[s + 1] = jnp.where(here, 0.0, rows[s + 1]) - tree([y[j] * w[j] for j in range(8)])
            g = list(w)
            for j in range(7, -1, -1):
                g[j] = g[j] * inv[j]
                for k in range(j):
                    g[k] = g[k] - low[j, k] * g[j]
            for i in range(s + 2, 16):
                part = tree([spread_column(rows[i], base + j) * g[j] for j in range(8)])
                rows[i] = jnp.where(here, 0.0, rows[i]) - part
        done = w[7]
        for i in range(6, -1, -1):
            done = jnp.where(sub <= i, w[i], done)
        x_ref[base:base + 8, :] = jnp.where(lane < base + 8, done, 0.0)


def block_factor(s_ref, x_ref, u_ref, z_ref, zero_ref, before, middle, after, later):
    def step(j, _):
        cj = pl.multiple_of(j * 128, 128)
        before(j)
        zero = zero_ref[...]
        rows = [s_ref[j, 8 * i:8 * i + 8, pl.ds(cj, 128)] for i in range(16)]
        if u_ref is not None:
            u_ref[j] = s_ref[j, :, pl.ds(cj, 128)]
        diag_factor(rows, zero, x_ref, lambda: middle(j))
        after(j)
        r_i = lax.broadcasted_iota(jnp.int32, (128, 128), 0)
        c_i = lax.broadcasted_iota(jnp.int32, (128, 128), 1)
        s_ref[j, :, pl.ds(cj, 128)] = (r_i == c_i).astype(jnp.float32)
        u = dot(left(x_ref[...]), right(s_ref[j]))
        s_ref[j] = u
        later(j)
        u = right(u)

        def trail(i, _):
            ci = pl.multiple_of(i * 128, 128)
            s_ref[i, :, pl.ds(cj, 128)] = jnp.zeros((128, 128), jnp.float32)
            s_ref[i] = s_ref[i] - dot(left(s_ref[j, :, pl.ds(ci, 128)].T), u)
            return 0

        lax.fori_loop(j + 1, 4, trail, 0)
        if z_ref is not None:
            lanes = lax.broadcasted_iota(jnp.int32, (128, 512), 1)
            inverse = jnp.where(lanes < (j + 1) * 128, s_ref[j, :, 0:512], 0.0)
            z_ref[...] += dot(left(inverse.T), u[:, 512:640])
        return 0

    if z_ref is not None:
        z_ref[...] = jnp.zeros_like(z_ref)
    lax.fori_loop(0, 4, step, 0)


def pick(condition):
    return jnp.where(condition, jnp.float32(1.0), jnp.float32(0.0))


def row_coefficients(maps, child, quarter):
    entries = [maps[t, quarter, child] for t in range(7)]
    same = [pick(entries[p] == p) if p < 7 else None for p in range(8)]
    above = [pick(entries[p - 1] == p) if p > 0 else None for p in range(8)]
    return same, above


def place(same, above, p, blocks):
    if p == 0:
        return blocks(0) * same[0]
    if p == 7:
        return blocks(6) * above[7]
    return blocks(p) * same[p] + blocks(p - 1) * above[p]


def kernel(
    update, own, maps_in, out,
    mine, theirs, own_mine, own_theirs, tile1, s1, a1, v_mine, v_theirs, z, x, u, head_mine, head_theirs, tile2, s2, a2, zero, land1, land2, maps,
    local, ex_s, ex_r, b1_s, b1_r, zx_s, zx_r, f1_s, f1_r, w1_s, w1_r, a1_s, a1_r, f2_s, f2_r, w2_s, w2_r, a2_s, a2_r, t_s, t_r,
):
    leaf, r, c = lax.axis_index("leaf"), lax.axis_index("frow"), lax.axis_index("fcol")
    core = lax.rem(leaf, 2)
    twin = leaf + 1 - 2 * core
    pair = leaf // 2
    other = pair + 1 - 2 * lax.rem(pair, 2)
    far = other * 2 + core
    cc, rc = pl.multiple_of(c * 128, 128), pl.multiple_of(r * 128, 128)
    h, g = pl.multiple_of(core * HALF, HALF), pl.multiple_of(HALF - core * HALF, HALF)
    upper = jnp.logical_or(jnp.logical_and(r <= c, c - r < 3), r - c == 3)
    early = jnp.logical_or(jnp.logical_and(r == 0, c < 3), r - c == 3)
    late = jnp.logical_and(upper, jnp.logical_not(early))
    plane = [(i, j) for i in range(4) for j in range(4) if (i, j) != (0, 0)]

    def at(i, j):
        return {"frow": lax.rem(r + i, 4), "fcol": lax.rem(c + j, 4)}

    def send(src, dst, s, t, to):
        return pltpu.make_async_remote_copy(
            src_ref=src, dst_ref=dst, send_sem=s, recv_sem=t, device_id=to, device_id_type=MESH
        )

    loads = [
        pltpu.make_async_copy(update.at[pl.ds(0, 1), pl.ds(h, HALF), pl.ds(0, 256)], mine.at[pl.ds(0, 1)], local.at[0]),
        pltpu.make_async_copy(own.at[:, pl.ds(h, HALF), :], own_mine, local.at[1]),
        pltpu.make_async_copy(maps_in, maps, local.at[3]),
        pltpu.make_async_copy(update.at[pl.ds(1, 6), pl.ds(h, HALF), pl.ds(0, 256)], mine.at[pl.ds(1, 6)], local.at[2]),
    ]
    for copy in loads:
        copy.start()

    barrier = pltpu.get_barrier_semaphore()
    pl.semaphore_signal(barrier, inc=1, device_id={"leaf": twin}, device_id_type=MESH)
    for i, j in plane:
        pl.semaphore_signal(barrier, inc=1, device_id=at(i, j), device_id_type=MESH)
    pl.semaphore_signal(barrier, inc=1, device_id={"leaf": far}, device_id_type=MESH)
    for ref in (zero, s1, s2):
        ref[...] = jnp.zeros_like(ref)
    pl.semaphore_wait(barrier, 17)

    swaps = [
        send(
            update.at[pl.ds(0, 1), pl.ds(g, HALF), pl.ds(0, 256)], theirs.at[pl.ds(0, 1)],
            ex_s.at[0], ex_r.at[0], {"leaf": twin},
        ),
        send(own.at[:, pl.ds(g, HALF), :], own_theirs, ex_s.at[1], ex_r.at[1], {"leaf": twin}),
        send(
            update.at[pl.ds(1, 6), pl.ds(g, HALF), pl.ds(0, 256)], theirs.at[pl.ds(1, 6)],
            ex_s.at[2], ex_r.at[2], {"leaf": twin},
        ),
    ]
    for copy in swaps:
        copy.start()

    loads[2].wait()
    sides = []
    for ref, child in ((mine, leaf), (theirs, twin)):
        same, above = row_coefficients(maps, child, r)
        first, second = maps[0, c, child], maps[1, c, child]
        sides.append((ref, same, above, pick(first == 0), pick(first == 1), pick(second == 1)))

    def front1(p, column):
        total = None
        for ref, same, above, none, one, two in sides:

            def blocks(t):
                left = ref[t, :, 0:128]
                if column == 0:
                    return left * none
                return left * one + ref[t, :, 128:256] * two

            part = place(same, above, p, blocks)
            total = part if total is None else total + part
        return total

    def spread(tile, store, s, t):
        return [
            send(tile, store.at[r, pl.ds(h, HALF), pl.ds(cc, 128)], s.at[4 * i + j], t.at[4 * r + c], at(i, j))
            for i, j in plane
        ]

    def start_spread(copies, when):
        @pl.when(when)
        def _():
            for copy in copies:
                copy.start()

    def finish_spread(copies):
        @pl.when(upper)
        def _():
            for copy in copies:
                copy.wait_send()

    def arrived(tile, store, s, t, i, j):
        @pl.when(jnp.logical_or(r != i, c != j))
        def _():
            send(
                tile, store.at[i, pl.ds(h, HALF), pl.ds(128 * j, 128)], s.at[4 * i + j], t.at[4 * i + j], at(0, 1)
            ).wait_recv()

    def twin_parts(store, s, t, width, offset):
        bounds = [(0, 0, 128), (0, 128, 384), (3, 0, 128), (1, 128, width), (2, 256, width), (3, 384, width)]
        if width > 512:
            bounds.insert(2, (0, 512, width))
        copies = []
        for n, (i, lo, hi) in enumerate(bounds):
            part = store.at[i, pl.ds(offset, HALF), pl.ds(lo, hi - lo)]
            copies.append(send(part, part, s.at[n], t.at[n], {"leaf": twin}))
        return copies

    def rows_out(store, s, t):
        block = store.at[:, pl.ds(cc, 128)]
        return [send(block, block, s.at[j], t.at[j], at(0, j)) for j in range(1, 4)]

    def rows_in(store, s, t):
        copies = []
        for j in range(1, 4):
            block = store.at[:, pl.ds(pl.multiple_of(lax.rem(c + 4 - j, 4) * 128, 128), 128)]
            copies.append(send(block, block, s.at[j], t.at[j], at(0, j)))
        return copies

    loads[0].wait()
    loads[1].wait()
    swaps[0].wait_recv()
    swaps[1].wait_recv()
    pivot = front1(0, 0) + (own_mine[0] + own_theirs[0])
    tile1[0] = pivot
    out1 = spread(tile1.at[0], land1, f1_s, f1_r)
    start_spread(out1, early)
    land1[r, pl.ds(h, HALF), pl.ds(cc, 128)] = pivot
    side = front1(0, 1)
    tile1[1] = side
    side1 = [
        send(tile1.at[1], land1.at[r, pl.ds(h, HALF), pl.ds(512, 128)], b1_s.at[i], b1_r.at[r], at(i, 0)) for i in range(1, 4)
    ]
    start_spread(side1, r == 0)
    land1[r, pl.ds(h, HALF), pl.ds(512, 128)] = side

    loads[3].wait()
    swaps[2].wait_recv()
    for p in range(1, 8):
        a1[HALF * (p - 1):HALF * p, pl.ds(cc, 128)] = front1(p, 0)
        v_mine[HALF * (p - 1):HALF * p, :] = front1(p, 1)
    start_spread(out1, late)
    start_spread(side1, r > 0)
    rows1 = rows_out(a1, a1_s, a1_r)

    def hooks(tile, store, sums, s, t, parts, width, side_arrived, rest):
        give, take = parts
        head = len(give) - 3
        groups = [((0, 1), (0, 2), (3, 0)), ((1, 1), (1, 2), (1, 3)), ((2, 2), (2, 3), (3, 3))]

        def arrive(group):
            for i, k in groups[group]:
                arrived(tile, store, s, t, i, k)

        def before(j):
            @pl.when(j == 0)
            def _():
                arrived(tile, store, s, t, 0, 0)
                give[0].start()
                take[0].wait_recv()
                sums[0, :, 0:128] = store[0, :, 0:128]

            for i in range(1, 4):
                def add(i=i):
                    take[head + i - 1].wait_recv()
                    sums[i, :, 128 * i:width] = sums[i, :, 128 * i:width] + store[i, :, 128 * i:width]

                pl.when(j == i)(add)

        def middle(j):
            @pl.when(j == 0)
            def _():
                arrive(0)
                side_arrived(0)
                for copy in give[1:head]:
                    copy.start()
                rest()

            @pl.when(j == 1)
            def _():
                arrive(2)
                side_arrived(2)
                side_arrived(3)
                for copy in give[head + 1:]:
                    copy.start()

        def after(j):
            @pl.when(j == 0)
            def _():
                for copy in take[1:head]:
                    copy.wait_recv()
                sums[0, :, 128:384] = store[0, :, 128:384]
                sums[0, :, 384:512] = store[3, :, 0:128].T
                if width > 512:
                    sums[0, :, 512:width] = store[0, :, 512:width]

        def later(j):
            @pl.when(j == 0)
            def _():
                arrive(1)
                side_arrived(1)
                give[head].start()

        return before, middle, after, later

    def side_arrived(i):
        @pl.when(r != i)
        def _():
            send(
                tile1.at[1], land1.at[i, pl.ds(h, HALF), pl.ds(512, 128)], b1_s.at[1], b1_r.at[i], at(1, 0)
            ).wait_recv()

    def nothing(i):
        return None

    def rows_out1():
        for copy in rows1:
            copy.start()

    parts1 = twin_parts(land1, w1_s, w1_r, 640, h), twin_parts(land1, w1_s, w1_r, 640, g)
    hooks1 = hooks(tile1.at[0], land1, s1, f1_s, f1_r, parts1, 640, side_arrived, rows_out1)
    block_factor(s1, x, None, z, zero, *hooks1)
    for copy in rows_in(a1, a1_s, a1_r):
        copy.wait_recv()

    sides2 = []
    for child, ref in ((32 + pair, v_mine), (32 + other, v_theirs)):
        same, above = row_coefficients(maps, child, r)
        sides2.append((ref, same, above, pick(maps[0, c, child] == 0)))

    z_right = right(z[...])
    v_mine[0:HALF, :] = v_mine[0:HALF, :] - dot(left(a1[0:HALF, :]), z_right)
    _, same, _, first = sides2[0]
    head_mine[...] = v_mine[0:HALF, :] * same[0] * first + (own_mine[1] + own_theirs[1])
    head = send(head_mine, head_theirs, zx_s.at[0], zx_r.at[0], {"leaf": far})
    head.start()
    v_mine[HALF:, :] = v_mine[HALF:, :] - dot(left(a1[HALF:, :]), z_right)
    rest = send(v_mine, v_theirs, zx_s.at[1], zx_r.at[1], {"leaf": far})
    rest.start()

    head.wait_recv()
    pivot = head_mine[...] + head_theirs[...]
    tile2[...] = pivot
    out2 = spread(tile2, land2, f2_s, f2_r)
    start_spread(out2, upper)
    land2[r, pl.ds(h, HALF), pl.ds(cc, 128)] = pivot
    rest.wait_recv()
    a2_own = a2.at[core]
    for p in range(1, 8):
        total = None
        for ref, same, above, first in sides2:
            part = place(same, above, p, lambda t: ref[HALF * t:HALF * t + HALF, :]) * first
            total = part if total is None else total + part
        a2[core, HALF * (p - 1):HALF * p, pl.ds(cc, 128)] = total
    rows2 = rows_out(a2_own, a2_s, a2_r)

    def rows_out2():
        for copy in rows2:
            copy.start()

    a2_give = send(a2_own, a2_own, t_s.at[0], t_r.at[0], {"leaf": twin})
    a2_twin = a2.at[1 - core]
    a2_take = send(a2_twin, a2_twin, t_s.at[0], t_r.at[0], {"leaf": twin})

    parts2 = twin_parts(land2, w2_s, w2_r, 512, h), twin_parts(land2, w2_s, w2_r, 512, g)
    before2, middle2, after2, later2 = hooks(tile2, land2, s2, f2_s, f2_r, parts2, 512, nothing, rows_out2)

    def middle2_rows(j):
        middle2(j)

        @pl.when(j == 3)
        def _():
            for copy in rows_in(a2_own, a2_s, a2_r):
                copy.wait_recv()
            a2_give.start()

    block_factor(s2, x, u, None, zero, before2, middle2_rows, after2, later2)

    lanes = lax.broadcasted_iota(jnp.int32, (128, 512), 1)
    inverse = right(jnp.where(lanes < (c + 1) * 128, s2[c], 0.0).T)

    def lower_rows(k):
        result = dot(left(a2[k]), inverse)
        k0 = pl.multiple_of(k * HALF, HALF)
        for p in range(7):
            out[p + 1, pl.ds(k0, HALF), :] = result[HALF * p:HALF * p + HALF, :]

    lower_rows(core)
    r_i = lax.broadcasted_iota(jnp.int32, (128, 128), 0)
    c_i = lax.broadcasted_iota(jnp.int32, (128, 128), 1)
    corner = jnp.where(r_i >= c_i, dot(left(u[c]), right(s2[c, :, pl.ds(cc, 128)].T)), 0.0)
    out[0] = s2[c, :, pl.ds(rc, 128)].T * pick(r > c) + corner * pick(r == c)
    a2_take.wait_recv()
    lower_rows(1 - core)
    a2_give.wait_send()
    for copy in swaps + side1 + rows1 + [head, rest] + rows2 + parts1[0] + parts2[0]:
        copy.wait_send()
    finish_spread(out1)
    finish_spread(out2)


def on_device(child_update, own_part, child_maps):
    shapes = [
        (7, 64, 256), (7, 64, 256), (2, 64, 128), (2, 64, 128), (2, 64, 128), (4, 128, 640), (448, 512), (448, 128), (448, 128),
        (512, 128), (128, 128), (4, 128, 128), (64, 128), (64, 128), (64, 128), (4, 128, 512), (2, 448, 512), (8, 128),
        (4, 128, 640), (4, 128, 512),
    ]
    sems = [4, 3, 3, 4, 4, 2, 2] + [16, 16, 7, 7, 4, 4] * 2 + [1, 1]
    panel = pl.pallas_call(
        kernel,
        out_shape=jax.ShapeDtypeStruct((8, 128, 128), jnp.float32),
        in_specs=[
            pl.BlockSpec(memory_space=pl.ANY),
            pl.BlockSpec(memory_space=pl.ANY),
            pl.BlockSpec(memory_space=pl.ANY),
        ],
        out_specs=pl.BlockSpec(memory_space=pltpu.VMEM),
        scratch_shapes=[pltpu.VMEM(s, jnp.float32) for s in shapes]
        + [pltpu.SMEM((7, 4, 48), jnp.int32)]
        + [pltpu.SemaphoreType.DMA((n,)) for n in sems],
        compiler_params=pltpu.CompilerParams(collective_id=0, has_side_effects=True, vmem_limit_bytes=62 << 20),
        name="merge",
    )(child_update[0].reshape(7, 128, 896), own_part[0], child_maps.transpose(2, 1, 0))
    return panel.reshape(1, 1024, 128)


def solution(mesh):
    in_specs = (P("leaf", "frow", "fcol"), P("leaf", None, "frow", "fcol"), P())
    out_specs = P("leaf", "frow", "fcol")
    return jax.shard_map(on_device, mesh=mesh, in_specs=in_specs, out_specs=out_specs, check_vma=False)
```

```python
import jax
import jax.numpy as jnp
from jax import lax
from jax.experimental import pallas as pl
from jax.experimental.pallas import tpu as pltpu
from jax.sharding import PartitionSpec as P

MESH = pl.DeviceIdType.MESH
HALF = 64


def thirds(v):
    high = v.astype(jnp.bfloat16)
    rest = v - high.astype(jnp.float32)
    middle = rest.astype(jnp.bfloat16)
    return high, middle, (rest - middle.astype(jnp.float32)).astype(jnp.bfloat16)


def left(v):
    h, m, l = thirds(v)
    return jnp.concatenate([h, h, m, h, m, l], 1)


def right(v):
    h, m, l = thirds(v)
    return jnp.concatenate([h, m, h, l, m, h], 0)


def dot(a, b):
    return lax.dot_general(a, b, (((1,), (0,)), ((), ())), preferred_element_type=jnp.float32)


def spread_column(v, j):
    return jnp.broadcast_to(v[:, j:j + 1], (8, 128))


def spread_row(v, j):
    return jnp.broadcast_to(v[j:j + 1, :], (8, 128))


def tree(terms):
    while len(terms) > 1:
        terms = [terms[i] + terms[i + 1] if i + 1 < len(terms) else terms[i] for i in range(0, len(terms), 2)]
    return terms[0]


def diag_factor(rows, zero, x_ref, middle):
    lane = lax.broadcasted_iota(jnp.int32, (8, 128), 1)
    sub = lax.broadcasted_iota(jnp.int32, (8, 128), 0)
    c = [spread_column(rows[0], j) + zero for j in range(8)]
    for s in range(16):
        if s == 8:
            middle()
        base = 8 * s
        here = (lane >= base) & (lane < base + 8)
        more = s < 15
        a = {(i, j): spread_row(c[j], i) for j in range(8) for i in range(j, 8)}
        unit = jnp.where(here, (lane - base == sub).astype(jnp.float32), rows[s])
        w = [spread_row(unit, j) for j in range(8)]
        if more:
            y = [spread_column(rows[s + 1], base + j) for j in range(8)]
            d = [spread_column(rows[s + 1], base + 8 + j) for j in range(8)]
        low, inv = {}, {}
        for j in range(8):
            inv[j] = lax.rsqrt(a[j, j])
            for i in range(j + 1, 8):
                low[i, j] = a[i, j] * inv[j]
            for k in range(j + 1, 8):
                for i in range(k, 8):
                    a[i, k] = a[i, k] - low[i, j] * low[k, j]
            w[j] = w[j] * inv[j]
            for k in range(j + 1, 8):
                w[k] = w[k] - low[k, j] * w[j]
            if more:
                y[j] = y[j] * inv[j]
                for k in range(j + 1, 8):
                    y[k] = y[k] - low[k, j] * y[j]
                for k in range(8):
                    d[k] = d[k] - y[j] * spread_row(y[j], k)
        if more:
            c = d
            rows[s + 1] = jnp.where(here, 0.0, rows[s + 1]) - tree([y[j] * w[j] for j in range(8)])
            g = list(w)
            for j in range(7, -1, -1):
                g[j] = g[j] * inv[j]
                for k in range(j):
                    g[k] = g[k] - low[j, k] * g[j]
            for i in range(s + 2, 16):
                part = tree([spread_column(rows[i], base + j) * g[j] for j in range(8)])
                rows[i] = jnp.where(here, 0.0, rows[i]) - part
        done = w[7]
        for i in range(6, -1, -1):
            done = jnp.where(sub <= i, w[i], done)
        x_ref[base:base + 8, :] = jnp.where(lane < base + 8, done, 0.0)


def block_factor(s_ref, x_ref, u_ref, z_ref, zero_ref, before, middle, after, later):
    def step(j, _):
        cj = pl.multiple_of(j * 128, 128)
        before(j)
        zero = zero_ref[...]
        rows = [s_ref[j, 8 * i:8 * i + 8, pl.ds(cj, 128)] for i in range(16)]
        if u_ref is not None:
            u_ref[j] = s_ref[j, :, pl.ds(cj, 128)]
        diag_factor(rows, zero, x_ref, lambda: middle(j))
        after(j)
        r_i = lax.broadcasted_iota(jnp.int32, (128, 128), 0)
        c_i = lax.broadcasted_iota(jnp.int32, (128, 128), 1)
        s_ref[j, :, pl.ds(cj, 128)] = (r_i == c_i).astype(jnp.float32)
        u = dot(left(x_ref[...]), right(s_ref[j]))
        s_ref[j] = u
        later(j)
        u = right(u)

        def trail(i, _):
            ci = pl.multiple_of(i * 128, 128)
            s_ref[i, :, pl.ds(cj, 128)] = jnp.zeros((128, 128), jnp.float32)
            s_ref[i] = s_ref[i] - dot(left(s_ref[j, :, pl.ds(ci, 128)].T), u)
            return 0

        lax.fori_loop(j + 1, 4, trail, 0)
        if z_ref is not None:
            lanes = lax.broadcasted_iota(jnp.int32, (128, 512), 1)
            inverse = jnp.where(lanes < (j + 1) * 128, s_ref[j, :, 0:512], 0.0)
            z_ref[...] += dot(left(inverse.T), u[:, 512:640])
        return 0

    if z_ref is not None:
        z_ref[...] = jnp.zeros_like(z_ref)
    lax.fori_loop(0, 4, step, 0)


def pick(condition):
    return jnp.where(condition, jnp.float32(1.0), jnp.float32(0.0))


def row_coefficients(maps, child, quarter):
    entries = [maps[t, quarter, child] for t in range(7)]
    same = [pick(entries[p] == p) if p < 7 else None for p in range(8)]
    above = [pick(entries[p - 1] == p) if p > 0 else None for p in range(8)]
    return same, above


def place(same, above, p, blocks):
    if p == 0:
        return blocks(0) * same[0]
    if p == 7:
        return blocks(6) * above[7]
    return blocks(p) * same[p] + blocks(p - 1) * above[p]


def kernel(
    update, own, maps_in, out,
    mine, theirs, own_mine, own_theirs, tile1, s1, a1, v_mine, v_theirs, z, x, u, head_mine, head_theirs, tile2, s2, a2, zero, land1, land2, maps,
    local, ex_s, ex_r, b1_s, b1_r, zx_s, zx_r, f1_s, f1_r, w1_s, w1_r, a1_s, a1_r, f2_s, f2_r, w2_s, w2_r, a2_s, a2_r, t_s, t_r,
):
    leaf, r, c = lax.axis_index("leaf"), lax.axis_index("frow"), lax.axis_index("fcol")
    core = lax.rem(leaf, 2)
    twin = leaf + 1 - 2 * core
    pair = leaf // 2
    other = pair + 1 - 2 * lax.rem(pair, 2)
    far = other * 2 + core
    cc, rc = pl.multiple_of(c * 128, 128), pl.multiple_of(r * 128, 128)
    h, g = pl.multiple_of(core * HALF, HALF), pl.multiple_of(HALF - core * HALF, HALF)
    upper = jnp.logical_or(jnp.logical_and(r <= c, c - r < 3), r - c == 3)
    early = jnp.logical_or(jnp.logical_and(r == 0, c < 3), r - c == 3)
    late = jnp.logical_and(upper, jnp.logical_not(early))
    plane = [(i, j) for i in (2, 1, 3, 0) for j in (2, 1, 3, 0) if (i, j) != (0, 0)]

    def at(i, j):
        return {"frow": lax.rem(r + i, 4), "fcol": lax.rem(c + j, 4)}

    def send(src, dst, s, t, to):
        return pltpu.make_async_remote_copy(
            src_ref=src, dst_ref=dst, send_sem=s, recv_sem=t, device_id=to, device_id_type=MESH
        )

    loads = [
        pltpu.make_async_copy(update.at[pl.ds(0, 1), pl.ds(h, HALF), pl.ds(0, 256)], mine.at[pl.ds(0, 1)], local.at[0]),
        pltpu.make_async_copy(own.at[:, pl.ds(h, HALF), :], own_mine, local.at[1]),
        pltpu.make_async_copy(maps_in, maps, local.at[3]),
        pltpu.make_async_copy(update.at[pl.ds(1, 6), pl.ds(h, HALF), pl.ds(0, 256)], mine.at[pl.ds(1, 6)], local.at[2]),
    ]
    for copy in loads:
        copy.start()

    barrier = pltpu.get_barrier_semaphore()
    pl.semaphore_signal(barrier, inc=1, device_id={"leaf": twin}, device_id_type=MESH)
    for i, j in plane:
        pl.semaphore_signal(barrier, inc=1, device_id=at(i, j), device_id_type=MESH)
    pl.semaphore_signal(barrier, inc=1, device_id={"leaf": far}, device_id_type=MESH)
    for ref in (zero, s1, s2):
        ref[...] = jnp.zeros_like(ref)
    pl.semaphore_wait(barrier, 17)

    swaps = [
        send(
            update.at[pl.ds(0, 1), pl.ds(g, HALF), pl.ds(0, 256)], theirs.at[pl.ds(0, 1)],
            ex_s.at[0], ex_r.at[0], {"leaf": twin},
        ),
        send(own.at[:, pl.ds(g, HALF), :], own_theirs, ex_s.at[1], ex_r.at[1], {"leaf": twin}),
        send(
            update.at[pl.ds(1, 6), pl.ds(g, HALF), pl.ds(0, 256)], theirs.at[pl.ds(1, 6)],
            ex_s.at[2], ex_r.at[2], {"leaf": twin},
        ),
    ]
    for copy in swaps:
        copy.start()

    loads[2].wait()
    sides = []
    for ref, child in ((mine, leaf), (theirs, twin)):
        same, above = row_coefficients(maps, child, r)
        first, second = maps[0, c, child], maps[1, c, child]
        sides.append((ref, same, above, pick(first == 0), pick(first == 1), pick(second == 1)))

    def front1(p, column):
        total = None
        for ref, same, above, none, one, two in sides:

            def blocks(t):
                left = ref[t, :, 0:128]
                if column == 0:
                    return left * none
                return left * one + ref[t, :, 128:256] * two

            part = place(same, above, p, blocks)
            total = part if total is None else total + part
        return total

    def spread(tile, store, s, t):
        return [
            send(tile, store.at[r, pl.ds(h, HALF), pl.ds(cc, 128)], s.at[4 * i + j], t.at[4 * r + c], at(i, j))
            for i, j in plane
        ]

    def start_spread(copies, when):
        @pl.when(when)
        def _():
            for copy in copies:
                copy.start()

    def finish_spread(copies):
        @pl.when(upper)
        def _():
            for copy in copies:
                copy.wait_send()

    def arrived(tile, store, s, t, i, j):
        @pl.when(jnp.logical_or(r != i, c != j))
        def _():
            send(
                tile, store.at[i, pl.ds(h, HALF), pl.ds(128 * j, 128)], s.at[4 * i + j], t.at[4 * i + j], at(0, 1)
            ).wait_recv()

    def twin_parts(store, s, t, width, offset):
        bounds = [(0, 0, 128), (0, 128, 384), (3, 0, 128), (1, 128, width), (2, 256, width), (3, 384, width)]
        if width > 512:
            bounds.insert(2, (0, 512, width))
        copies = []
        for n, (i, lo, hi) in enumerate(bounds):
            part = store.at[i, pl.ds(offset, HALF), pl.ds(lo, hi - lo)]
            copies.append(send(part, part, s.at[n], t.at[n], {"leaf": twin}))
        return copies

    def rows_out(store, s, t):
        block = store.at[:, pl.ds(cc, 128)]
        return [send(block, block, s.at[j], t.at[j], at(0, j)) for j in range(1, 4)]

    def rows_in(store, s, t):
        copies = []
        for j in range(1, 4):
            block = store.at[:, pl.ds(pl.multiple_of(lax.rem(c + 4 - j, 4) * 128, 128), 128)]
            copies.append(send(block, block, s.at[j], t.at[j], at(0, j)))
        return copies

    loads[0].wait()
    loads[1].wait()
    swaps[0].wait_recv()
    swaps[1].wait_recv()
    pivot = front1(0, 0) + (own_mine[0] + own_theirs[0])
    tile1[0] = pivot
    out1 = spread(tile1.at[0], land1, f1_s, f1_r)
    start_spread(out1, early)
    land1[r, pl.ds(h, HALF), pl.ds(cc, 128)] = pivot
    side = front1(0, 1)
    tile1[1] = side
    side1 = [
        send(tile1.at[1], land1.at[r, pl.ds(h, HALF), pl.ds(512, 128)], b1_s.at[i], b1_r.at[r], at(i, 0)) for i in range(1, 4)
    ]
    start_spread(side1, r == 0)
    land1[r, pl.ds(h, HALF), pl.ds(512, 128)] = side

    loads[3].wait()
    swaps[2].wait_recv()
    for p in range(1, 8):
        a1[HALF * (p - 1):HALF * p, pl.ds(cc, 128)] = front1(p, 0)
        v_mine[HALF * (p - 1):HALF * p, :] = front1(p, 1)
    start_spread(out1, late)
    start_spread(side1, r > 0)
    rows1 = rows_out(a1, a1_s, a1_r)

    def hooks(tile, store, sums, s, t, parts, width, side_arrived, rest):
        give, take = parts
        head = len(give) - 3
        groups = [((0, 1), (0, 2), (3, 0)), ((1, 1), (1, 2), (1, 3)), ((2, 2), (2, 3), (3, 3))]

        def arrive(group):
            for i, k in groups[group]:
                arrived(tile, store, s, t, i, k)

        def before(j):
            @pl.when(j == 0)
            def _():
                arrived(tile, store, s, t, 0, 0)
                give[0].start()
                take[0].wait_recv()
                sums[0, :, 0:128] = store[0, :, 0:128]

            for i in range(1, 4):
                def add(i=i):
                    take[head + i - 1].wait_recv()
                    sums[i, :, 128 * i:width] = sums[i, :, 128 * i:width] + store[i, :, 128 * i:width]

                pl.when(j == i)(add)

        def middle(j):
            @pl.when(j == 0)
            def _():
                arrive(0)
                side_arrived(0)
                for copy in give[1:head]:
                    copy.start()
                rest()

            @pl.when(j == 1)
            def _():
                arrive(2)
                side_arrived(2)
                side_arrived(3)
                for copy in give[head + 1:]:
                    copy.start()

        def after(j):
            @pl.when(j == 0)
            def _():
                for copy in take[1:head]:
                    copy.wait_recv()
                sums[0, :, 128:384] = store[0, :, 128:384]
                sums[0, :, 384:512] = store[3, :, 0:128].T
                if width > 512:
                    sums[0, :, 512:width] = store[0, :, 512:width]

        def later(j):
            @pl.when(j == 0)
            def _():
                arrive(1)
                side_arrived(1)
                give[head].start()

        return before, middle, after, later

    def side_arrived(i):
        @pl.when(r != i)
        def _():
            send(
                tile1.at[1], land1.at[i, pl.ds(h, HALF), pl.ds(512, 128)], b1_s.at[1], b1_r.at[i], at(1, 0)
            ).wait_recv()

    def nothing(i):
        return None

    def rows_out1():
        for copy in rows1:
            copy.start()

    parts1 = twin_parts(land1, w1_s, w1_r, 640, h), twin_parts(land1, w1_s, w1_r, 640, g)
    hooks1 = hooks(tile1.at[0], land1, s1, f1_s, f1_r, parts1, 640, side_arrived, rows_out1)
    block_factor(s1, x, None, z, zero, *hooks1)
    for copy in rows_in(a1, a1_s, a1_r):
        copy.wait_recv()

    sides2 = []
    for child, ref in ((32 + pair, v_mine), (32 + other, v_theirs)):
        same, above = row_coefficients(maps, child, r)
        sides2.append((ref, same, above, pick(maps[0, c, child] == 0)))

    z_right = right(z[...])
    v_mine[0:HALF, :] = v_mine[0:HALF, :] - dot(left(a1[0:HALF, :]), z_right)
    _, same, _, first = sides2[0]
    head_mine[...] = v_mine[0:HALF, :] * same[0] * first + (own_mine[1] + own_theirs[1])
    head = send(head_mine, head_theirs, zx_s.at[0], zx_r.at[0], {"leaf": far})
    head.start()
    v_mine[HALF:, :] = v_mine[HALF:, :] - dot(left(a1[HALF:, :]), z_right)
    rest = send(v_mine, v_theirs, zx_s.at[1], zx_r.at[1], {"leaf": far})
    rest.start()

    head.wait_recv()
    pivot = head_mine[...] + head_theirs[...]
    tile2[...] = pivot
    out2 = spread(tile2, land2, f2_s, f2_r)
    start_spread(out2, upper)
    land2[r, pl.ds(h, HALF), pl.ds(cc, 128)] = pivot
    rest.wait_recv()
    a2_own = a2.at[core]
    for p in range(1, 8):
        total = None
        for ref, same, above, first in sides2:
            part = place(same, above, p, lambda t: ref[HALF * t:HALF * t + HALF, :]) * first
            total = part if total is None else total + part
        a2[core, HALF * (p - 1):HALF * p, pl.ds(cc, 128)] = total
    rows2 = rows_out(a2_own, a2_s, a2_r)

    def rows_out2():
        for copy in rows2:
            copy.start()

    a2_give = send(a2_own, a2_own, t_s.at[0], t_r.at[0], {"leaf": twin})
    a2_twin = a2.at[1 - core]
    a2_take = send(a2_twin, a2_twin, t_s.at[0], t_r.at[0], {"leaf": twin})

    parts2 = twin_parts(land2, w2_s, w2_r, 512, h), twin_parts(land2, w2_s, w2_r, 512, g)
    before2, middle2, after2, later2 = hooks(tile2, land2, s2, f2_s, f2_r, parts2, 512, nothing, rows_out2)

    def before2_rows(j):
        before2(j)

        @pl.when(j == 3)
        def _():
            for copy in rows_in(a2_own, a2_s, a2_r):
                copy.wait_recv()
            a2_give.start()

    block_factor(s2, x, u, None, zero, before2_rows, middle2, after2, later2)

    lanes = lax.broadcasted_iota(jnp.int32, (128, 512), 1)
    inverse = right(jnp.where(lanes < (c + 1) * 128, s2[c], 0.0).T)

    def lower_rows(k):
        result = dot(left(a2[k]), inverse)
        k0 = pl.multiple_of(k * HALF, HALF)
        for p in range(7):
            out[p + 1, pl.ds(k0, HALF), :] = result[HALF * p:HALF * p + HALF, :]

    lower_rows(core)
    r_i = lax.broadcasted_iota(jnp.int32, (128, 128), 0)
    c_i = lax.broadcasted_iota(jnp.int32, (128, 128), 1)
    corner = jnp.where(r_i >= c_i, dot(left(u[c]), right(s2[c, :, pl.ds(cc, 128)].T)), 0.0)
    out[0] = s2[c, :, pl.ds(rc, 128)].T * pick(r > c) + corner * pick(r == c)
    a2_take.wait_recv()
    lower_rows(1 - core)
    a2_give.wait_send()
    for copy in swaps + side1 + rows1 + [head, rest] + rows2 + parts1[0] + parts2[0]:
        copy.wait_send()
    finish_spread(out1)
    finish_spread(out2)


def on_device(child_update, own_part, child_maps):
    shapes = [
        (7, 64, 256), (7, 64, 256), (2, 64, 128), (2, 64, 128), (2, 64, 128), (4, 128, 640), (448, 512), (448, 128), (448, 128),
        (512, 128), (128, 128), (4, 128, 128), (64, 128), (64, 128), (64, 128), (4, 128, 512), (2, 448, 512), (8, 128),
        (4, 128, 640), (4, 128, 512),
    ]
    sems = [4, 3, 3, 4, 4, 2, 2] + [16, 16, 7, 7, 4, 4] * 2 + [1, 1]
    panel = pl.pallas_call(
        kernel,
        out_shape=jax.ShapeDtypeStruct((8, 128, 128), jnp.float32),
        in_specs=[
            pl.BlockSpec(memory_space=pl.ANY),
            pl.BlockSpec(memory_space=pl.ANY),
            pl.BlockSpec(memory_space=pl.ANY),
        ],
        out_specs=pl.BlockSpec(memory_space=pltpu.VMEM),
        scratch_shapes=[pltpu.VMEM(s, jnp.float32) for s in shapes]
        + [pltpu.SMEM((7, 4, 48), jnp.int32)]
        + [pltpu.SemaphoreType.DMA((n,)) for n in sems],
        compiler_params=pltpu.CompilerParams(collective_id=0, has_side_effects=True, vmem_limit_bytes=62 << 20),
        name="merge",
    )(child_update[0].reshape(7, 128, 896), own_part[0], child_maps.transpose(2, 1, 0))
    return panel.reshape(1, 1024, 128)


def solution(mesh):
    in_specs = (P("leaf", "frow", "fcol"), P("leaf", None, "frow", "fcol"), P())
    out_specs = P("leaf", "frow", "fcol")
    return jax.shard_map(on_device, mesh=mesh, in_specs=in_specs, out_specs=out_specs, check_vma=False)
```
